128 devices in a mesh: lat: 16 (over x, z), lon: 8 (over y, core).
Axes of the slice: x: 4, y: 4, z: 4, core: 2. Of those that a mesh axis runs over, the one named last changes fastest.
Arguments:
- control: float32 [16, 1024, 7200], P(None, 'lat', 'lon'), may hold values from -6 to 6
- inverse: float32 [32, 16, 32, 32], P('lat'), may hold values from -1 to 2
- coupling: float32 [16], replicated, may hold values from 0.2 to 1
- jacobian: float32 [16, 128], replicated, may hold values from -1.5 to 1.5
- error_weight: float32 [128], replicated, may hold values from 0.2 to 2
- response: float32 [512], replicated, may hold values from 1 to 10
- obs_values: float32 [262144, 128], P(('lat', 'lon')), may hold values from -6 to 6
- obs_tile: int32 [262144, 1], P(('lat', 'lon')), may hold values from 0 to 127; in each aligned block of 2048 rows (0 to 2047, 2048 to 4095, ...) at most 32 rows name the same one
- obs_points: int32 [262144, 4], P(('lat', 'lon')), may hold values from 0 to 57599
- obs_weights: float32 [262144, 4], P(('lat', 'lon')), may hold values from 0.1 to 1
- live_rows: int32 [128], P(('lat', 'lon')), may hold values from 1536 to 2048, as said below
Outputs:
- state: float32 [16, 1024, 7200], P(None, 'lat', 'lon')
- gradient: float32 [16, 1024, 7200], P(None, 'lat', 'lon')
- direction: float32 [16, 1024, 7200], P(None, 'lat', 'lon')
The draws below stay inside these ranges and needn't reach their ends.
Inputs may be any that keep to these rules, and one draw needn't show every extreme that they name: `obs_tile`: no tile is named by more than 32 rows of one device's list; in every draw some device's list names some tile exactly 32 times. `obs_points`: cell index within the named tile, row-major over 64 latitudes and 900 longitudes. `live_rows`: some device has all 2048 rows live in every draw.
All inputs are finite; a program needn't handle non-finite values.
Results may differ from the reference program's by a relative error of at most 0.0001.
Values sent between devices are 32-bit elements; how exact they have to be, the bound alone decides.
No kernel may reach another device: no remote copies, remote signals or barrier semaphores. Data moves between devices by JAX's collectives and lax.ppermute only.
A program may use at most 192 MiB of HBM per device.

```python
import math
import jax
import jax.numpy as jnp
import numpy as np
from jax import lax

CH = 16
NLON = 7200
KEEP = 512
CHANNELS = 128
BLOCK_LATITUDES = 32
STEPS = 2
RLAT = 64
OBS_DEV = 2048
NLAT = 1024
CLON = 900
TILES = 128
TILES_PER_CIRCLE = 8
OBS = 262144
CAP = 32


def draw_inverse(key, part):
    key = jax.random.fold_in(key, 5)
    key_noise, key_diag = jax.random.split(key)
    shape_all = (NLAT // BLOCK_LATITUDES, CH, BLOCK_LATITUDES, BLOCK_LATITUDES)
    noise_part = jnp.clip(jax.random.normal(key_noise, shape_all, jnp.float32), -3.0, 3.0)
    diagonal = jax.random.uniform(key_diag, shape_all[:3], jnp.float32, 0.8, 1.2)
    identity = jnp.eye(BLOCK_LATITUDES, dtype=jnp.float32)
    return noise_part * (0.5 / math.sqrt(BLOCK_LATITUDES)) + diagonal[..., None] * identity


def draw_live_rows(key, part):
    key = jax.random.fold_in(key, 7)
    key_count, key_full = jax.random.split(key)
    counts = jax.random.randint(key_count, (TILES,), OBS_DEV * 3 // 4, OBS_DEV + 1, dtype=jnp.int32)
    fullest = jax.random.randint(key_full, (), 0, TILES, dtype=jnp.int32)
    return counts.at[fullest].set(OBS_DEV)


def plant(drawn, key, smallest, top_value):
    extent = drawn.shape
    index_at = [jax.random.randint(jax.random.fold_in(key, axis), (), 0, extent[axis]) for axis in range(len(extent))]
    drawn = drawn.at[tuple(index_at)].set(smallest)
    longest = extent.index(max(extent))
    index_at[longest] = (index_at[longest] + 1) % extent[longest]
    return drawn.at[tuple(index_at)].set(top_value)


def level_of(own_key, extent, cuts, least, high):
    level = 1.0
    for axis_at, parts in cuts:
        heights = jax.random.uniform(jax.random.fold_in(jax.random.fold_in(own_key, 6), axis_at), (parts,), jnp.float32, least / len(cuts), high / len(cuts))
        level = level * jnp.repeat(jnp.exp(heights), extent[axis_at] // parts).reshape((-1,) + (1,) * (len(extent) - 1 - axis_at))
    return level


def routed_block(rng, own, number, rows, count, top, most, slope):
    ranking = jax.random.permutation(rng, count)
    packed, ordinary = load_shares(count, rows * top, most, slope, True), load_shares(count, rows * top, most, slope, False)
    places = jnp.arange(count)

    def named(sizes, rotation):
        used = int((sizes > 0).sum())
        fixed = max(1, used // 4)
        shifted = fixed + (places - fixed + rotation * (used - fixed)) % max(1, count - fixed)
        return jnp.zeros((count,), jnp.int32).at[ranking[jnp.where(places < fixed, places, shifted)]].set(jnp.asarray(sizes, jnp.int32))

    sizes = jnp.where(number % 4 == 0, named(packed, number // 4), named(ordinary, number - number // 4 - 1))
    mixed = jax.random.permutation(jax.random.fold_in(own, 3), count)
    giver, sink = mixed[0:count // 2 * 2:2], mixed[1:count // 2 * 2:2]
    slack = jnp.minimum(sizes[giver] - 1, most - sizes[sink]) // 2
    slack = jnp.where((giver == ranking[0]) | (sink == ranking[0]) | (sizes[sink] == 0), 0, jnp.maximum(slack, 0))
    shifted = jax.random.randint(jax.random.fold_in(own, 4), (count // 2,), 0, 1 << 20) % (slack + 1)
    sizes = sizes.at[giver].add(-shifted).at[sink].add(shifted)
    members = jnp.searchsorted(jnp.cumsum(sizes), jnp.arange(rows * top), side="right").astype(jnp.int32)
    grid = members.reshape(top, rows).T
    grid = grid[jax.random.permutation(jax.random.fold_in(own, 1), rows)]
    rotation = jax.random.randint(jax.random.fold_in(own, 2), (rows, 1), 0, top)
    return jnp.take_along_axis(grid, (jnp.arange(top)[None, :] + rotation) % top, axis=1)


def load_shares(number_of, total, most, lean, full):
    weights = [(1 << 20) // math.isqrt(rank ** lean) + 1 for rank in range(1, number_of + 1)]
    largest = most if full else min(most, max(-(-total // number_of), total * weights[0] // sum(weights)))
    least = 1 if total - largest >= number_of - 1 else 0
    given, rest = [largest] + [least] * (number_of - 1), total - largest - least * (number_of - 1)
    while rest > 0:
        movable = [i for i in range(1, number_of) if given[i] < largest] or [i for i in range(1, number_of) if given[i] < most]
        pool, budget = sum([weights[i] for i in movable]), rest
        for i in movable:
            more = min(most - given[i], max(1, budget * weights[i] // pool), rest)
            given[i] = given[i] + more
            rest = rest - more
    return np.array(given)


def noise(stream_key, shape, scale, limit, pieces=(), kind=jnp.bfloat16):
    array = jax.random.normal(stream_key, shape, jnp.float32) * scale
    if len(pieces) > 0:
        array = level_of(stream_key, shape, pieces, -0.22, 0.18) * array
    return jnp.clip(array, min=-limit, max=limit).astype(kind)


def setup_inputs(seed: int = 0) -> dict:
    streams_of = jax.random.split(jax.random.key(seed), 12)
    control = noise(streams_of[0], (CH, NLAT, NLON), 1.0, 6.0, ((1, 16), (2, 8)), jnp.float32)
    inverse = draw_inverse(jax.random.fold_in(streams_of[11], 71), 0)
    coupling = jnp.clip(jnp.exp(jax.random.uniform(streams_of[2], (CH,), jnp.float32, math.log(0.2), math.log(1.0))), 0.2, 1.0)
    jacobian = noise(streams_of[3], (CH, CHANNELS), CH ** -0.5, 1.5, (), jnp.float32)
    error_weight = jnp.clip(jnp.exp(jax.random.uniform(streams_of[4], (CHANNELS,), jnp.float32, math.log(0.2), math.log(2.0))), 0.2, 2.0)
    response = jnp.clip(jnp.exp(jax.random.uniform(streams_of[5], (KEEP,), jnp.float32, math.log(1.0), math.log(10.0))), 1.0, 10.0)
    obs_values = noise(streams_of[6], (OBS, CHANNELS), 1.0, 6.0, ((0, 128),), jnp.float32)
    obs_tile_keys = jax.random.split(jax.random.fold_in(streams_of[7], 1), OBS // OBS_DEV)
    obs_tile_turns = jax.random.permutation(jax.random.fold_in(streams_of[7], 3), OBS // OBS_DEV)
    obs_tile = jax.vmap(lambda own, number: routed_block(jax.random.fold_in(streams_of[7], 2), own, number, OBS_DEV, TILES, 1, CAP, 1))(obs_tile_keys, obs_tile_turns).reshape((OBS, 1))
    obs_points = plant(jax.random.randint(streams_of[8], (OBS, 4), 0, RLAT * CLON), jax.random.fold_in(streams_of[8], 1), 0, (RLAT * CLON) - 1).astype(jnp.int32)
    obs_weights = jnp.clip(0.1 + 0.9 * jax.random.uniform(streams_of[9], (OBS, 4), jnp.float32) ** level_of(streams_of[9], (OBS, 4), ((0, 128),), -0.2, 0.2), 0.1, 1.0)
    live_rows = draw_live_rows(jax.random.fold_in(streams_of[11], 71), 0)
    return {"control": control, "inverse": inverse, "coupling": coupling, "jacobian": jacobian, "error_weight": error_weight, "response": response, "obs_values": obs_values, "obs_tile": obs_tile, "obs_points": obs_points, "obs_weights": obs_weights, "live_rows": live_rows}


MATMUL_ACCURACY = lax.Precision.HIGHEST


def shift_edges(field):
    row_count = field.shape[1]
    padded = jnp.pad(field, ((0, 0), (1, 1), (0, 0)))
    return padded[:, 0:row_count:BLOCK_LATITUDES], padded[:, BLOCK_LATITUDES + 1::BLOCK_LATITUDES]


def smooth_forward(field, inverse, coupling):
    channels, row_count, cols = field.shape
    northern_row, southern_row = shift_edges(field)
    blocks = field.reshape(channels, row_count // BLOCK_LATITUDES, BLOCK_LATITUDES, cols)
    coupled_rows = coupling[:, None, None]
    right_side = blocks.at[:, :, 0].add(coupled_rows * northern_row).at[:, :, BLOCK_LATITUDES - 1].add(coupled_rows * southern_row)
    return jnp.einsum('bcij,cbjn->cbin', inverse, right_side, precision=MATMUL_ACCURACY).reshape(field.shape)


def smooth_adjoint(field, inverse, coupling):
    channels, row_count, cols = field.shape
    blocks = field.reshape(channels, row_count // BLOCK_LATITUDES, BLOCK_LATITUDES, cols)
    mixed = jnp.einsum('bcji,cbjn->cbin', inverse, blocks, precision=MATMUL_ACCURACY)
    northern_row, southern_row = shift_edges(mixed.reshape(field.shape))
    coupled_rows = coupling[:, None, None]
    result = mixed.at[:, :, 0].add(coupled_rows * northern_row).at[:, :, BLOCK_LATITUDES - 1].add(coupled_rows * southern_row)
    return result.reshape(field.shape)


def zonal_filter(field, response):
    spectrum = jnp.fft.rfft(field, axis=-1)[..., :KEEP] * response
    return jnp.fft.irfft(spectrum, n=NLON, axis=-1).astype(field.dtype)


def reference(control, inverse, coupling, jacobian, error_weight, response, obs_values, obs_tile, obs_points, obs_weights, live_rows):
    state = control
    for step_index in range(STEPS):
        state = smooth_forward(state, inverse, coupling)
    source = jnp.arange(OBS, dtype=jnp.int32) // OBS_DEV
    position = jnp.arange(OBS, dtype=jnp.int32) % OBS_DEV
    live_mask = (position < live_rows[source]).astype(obs_weights.dtype)
    weights_live = obs_weights * live_mask[:, None]
    target = obs_tile[:, 0]
    lat_cell = (target // TILES_PER_CIRCLE)[:, None] * RLAT + obs_points // CLON
    lon_cell = (target % TILES_PER_CIRCLE)[:, None] * CLON + obs_points % CLON
    flat_index = (lat_cell * NLON + lon_cell).astype(jnp.int32)
    cell_values = state.reshape(CH, -1).T
    interp = jnp.einsum('op,opc->oc', weights_live, cell_values[flat_index], precision=MATMUL_ACCURACY)
    model_obs = jnp.dot(interp, jacobian, precision=MATMUL_ACCURACY)
    adjoint_cols = jnp.dot((model_obs - obs_values) * error_weight, jacobian.T, precision=MATMUL_ACCURACY)
    spread = weights_live[:, :, None] * adjoint_cols[:, None, :]
    adjoint_cells = jnp.zeros_like(cell_values).at[flat_index].add(spread)
    adjoint = adjoint_cells.T.reshape(state.shape)
    for step_index in range(STEPS):
        adjoint = smooth_adjoint(adjoint, inverse, coupling)
    gradient = control + adjoint
    direction = zonal_filter(gradient, response)
    return state, gradient, direction
```

```python
import functools

import jax
import jax.numpy as jnp
import numpy as np
from jax import lax
from jax.experimental import pallas as pl
from jax.experimental.pallas import tpu as pltpu
from jax.sharding import PartitionSpec as P

CH = 16
KEEP = 512
NLON = 7200
CLON = 900
RLAT = 64
HALF = 32
SLOTS = 32
TILES = 128
ROWS = 2048
LANES = 128
WORDS = LANES + SLOTS * 32
CELL_ROWS = 8 * 1024
ACCS = 4
F32 = jnp.float32
BF16 = jnp.bfloat16
EXACT = lax.Precision.HIGHEST
VMEM_BYTES = 60 * 1024 * 1024
VM = pl.BlockSpec(memory_space=pltpu.VMEM)
SM = pl.BlockSpec(memory_space=pltpu.SMEM)


def params():
    return pltpu.CompilerParams(vmem_limit_bytes=VMEM_BYTES)


def split(x):
    head = x.astype(BF16)
    return head, (x - head.astype(F32)).astype(BF16)


def mm(a, b):
    return jnp.dot(a, b, preferred_element_type=F32)


def mm_tn(a, b):
    return lax.dot_general(a, b, (((0,), (0,)), ((), ())), preferred_element_type=F32)


def dot3(a, b):
    a_head, a_tail = split(a)
    b_head, b_tail = split(b)
    rows = a.shape[0]
    both = mm(jnp.concatenate([a_head, a_tail], axis=0), b_head)
    return both[:rows] + both[rows:] + mm(a_head, b_tail)


def base_tables():
    longitude = np.arange(CLON)[:, None]
    wavenumber = np.arange(KEEP)[None, :]
    phase = 2.0 * np.pi * ((longitude * wavenumber) % NLON) / NLON
    table = np.concatenate([np.cos(phase), np.sin(phase)], axis=1).astype(np.float32)
    return table, np.ascontiguousarray(table.T)


def turn_tables():
    tile = np.arange(8)[:, None]
    wavenumber = np.arange(KEEP)[None, :]
    phase = 2.0 * np.pi * ((tile * wavenumber) % 8) / 8
    return np.stack([np.cos(phase), np.sin(phase)], axis=1).astype(np.float32)


def table_kernel(base_ref, across_ref, row_ref, col_ref, head_ref, tail_ref, head_t_ref, tail_t_ref):
    turn_cos = row_ref[0:1, :]
    turn_sin = row_ref[1:2, :]
    cos = base_ref[:, :KEEP]
    sin = base_ref[:, KEEP:]
    for part, value in ((0, cos * turn_cos - sin * turn_sin), (1, sin * turn_cos + cos * turn_sin)):
        head, tail = split(value)
        head_ref[:, part * KEEP : (part + 1) * KEEP] = head
        tail_ref[:, part * KEEP : (part + 1) * KEEP] = tail
    turn_cos = col_ref[:, 0:1]
    turn_sin = col_ref[:, 1:2]
    cos = across_ref[:KEEP, :]
    sin = across_ref[KEEP:, :]
    for part, value in ((0, cos * turn_cos - sin * turn_sin), (1, sin * turn_cos + cos * turn_sin)):
        head, tail = split(value)
        head_t_ref[part * KEEP : (part + 1) * KEEP, :] = head
        tail_t_ref[part * KEEP : (part + 1) * KEEP, :] = tail


def make_tables(lon):
    base, across = base_tables()
    turns = lax.dynamic_index_in_dim(jnp.asarray(turn_tables()), lon, 0, keepdims=False)
    return pl.pallas_call(
        table_kernel,
        out_shape=(
            jax.ShapeDtypeStruct((CLON, 2 * KEEP), BF16),
            jax.ShapeDtypeStruct((CLON, 2 * KEEP), BF16),
            jax.ShapeDtypeStruct((2 * KEEP, CLON), BF16),
            jax.ShapeDtypeStruct((2 * KEEP, CLON), BF16),
        ),
        in_specs=[VM] * 4,
        out_specs=[VM] * 4,
        compiler_params=params(),
        name="tables",
    )(jnp.asarray(base), jnp.asarray(across), turns, turns.T)


def band_matrices(inverse, coupling):
    zero = jnp.zeros((CH, HALF, HALF), F32)
    blocks = jnp.concatenate(
        [jnp.concatenate([inverse[0], zero], axis=2), jnp.concatenate([zero, inverse[1]], axis=2)], axis=1
    )
    c = coupling[:, None, None]
    column = jnp.arange(RLAT)[None, None, :]
    step = blocks + c * (
        jnp.where(column == HALF, blocks[:, :, HALF - 1 : HALF], 0.0)
        + jnp.where(column == HALF - 1, blocks[:, :, HALF : HALF + 1], 0.0)
    )
    first, last = blocks[:, :, 0:1], blocks[:, :, RLAT - 1 : RLAT]
    products = jnp.einsum(
        "cij,cjk->cik", step, jnp.concatenate([step, first, last], axis=2), precision=EXACT
    )
    twice, step_first, step_last = products[:, :, :RLAT], products[:, :, RLAT : RLAT + 1], products[:, :, RLAT + 1 :]
    pad = jnp.zeros((CH, RLAT, 6), F32)
    forward = jnp.concatenate([twice, c * step_first, c * first, pad, c * step_last, c * last, pad], axis=2)
    backward = jnp.concatenate([twice, first, step_first, pad, last, step_last, pad], axis=2)
    row = jnp.arange(RLAT)[None, :, None]
    first_unit = jnp.broadcast_to((row == 0).astype(F32), (CH, RLAT, 1))
    last_unit = jnp.broadcast_to((row == RLAT - 1).astype(F32), (CH, RLAT, 1))
    top_row = jnp.swapaxes(step[:, 0:1, :], 1, 2)
    bottom_row = jnp.swapaxes(step[:, RLAT - 1 :, :], 1, 2)
    edges = jnp.concatenate([first_unit, top_row, pad, last_unit, bottom_row, pad], axis=2)
    mend = jnp.concatenate([c * top_row, c * first_unit, pad, c * bottom_row, c * last_unit, pad], axis=2)
    alpha = jnp.concatenate([c * blocks[:, 0:1, 0:1], c * blocks[:, RLAT - 1 :, RLAT - 1 :]], axis=2)
    place = jnp.arange(16)[None, :, None]
    alpha_rows = jnp.where(place == 2, alpha[:, :, 0:1], 0.0) + jnp.where(place == 10, alpha[:, :, 1:2], 0.0)
    return forward, backward, jnp.swapaxes(edges, 1, 2), mend, alpha_rows


def edges_kernel(field_ref, edges_ref, alpha_ref, north_ref, south_ref):
    for channel in range(CH):
        rows = dot3(edges_ref[channel], field_ref[channel]) + alpha_ref[channel]
        north_ref[channel] = rows[:8]
        south_ref[channel] = rows[8:]


def send_edges(north, south):
    count = lax.axis_size("lat")
    from_south = lax.ppermute(north, "lat", [(i + 1, i) for i in range(count - 1)])
    from_north = lax.ppermute(south, "lat", [(i, i + 1) for i in range(count - 1)])
    return from_north, from_south


def forward_kernel(field_ref, north_ref, south_ref, matrix_ref, state_ref, cells_ref):
    column = lax.broadcasted_iota(jnp.int32, (RLAT, 80), 1)
    for channel in range(CH):
        matrix = matrix_ref[channel]
        alpha_north = north_ref[channel, 2:3, 0:1]
        alpha_south = south_ref[channel, 2:3, 0:1]
        matrix = (
            matrix
            + jnp.where(column == 0, matrix[:, 65:66] * alpha_north, 0.0)
            + jnp.where(column == RLAT - 1, matrix[:, 73:74] * alpha_south, 0.0)
        )
        field = jnp.concatenate([field_ref[channel], north_ref[channel], south_ref[channel]], axis=0)
        state_ref[channel] = dot3(matrix, field)
    for group in range(8):
        for lane_tile in range(2):
            lanes = slice(lane_tile * LANES, (lane_tile + 1) * LANES)
            piece = state_ref[:, group * 8 : (group + 1) * 8, lanes].reshape(LANES, LANES)
            cells_ref[group, lanes, :] = piece.T


def forward_diffusion(control, from_north, from_south, forward):
    width = 256
    return pl.pallas_call(
        forward_kernel,
        grid=(4,),
        out_shape=(
            jax.ShapeDtypeStruct((CH, RLAT, CLON), F32),
            jax.ShapeDtypeStruct((8, 1024, LANES), F32),
        ),
        in_specs=[
            pl.BlockSpec((CH, RLAT, width), lambda i: (0, 0, i)),
            pl.BlockSpec((CH, 8, width), lambda i: (0, 0, i)),
            pl.BlockSpec((CH, 8, width), lambda i: (0, 0, i)),
            pl.BlockSpec((CH, RLAT, 80), lambda i: (0, 0, 0)),
        ],
        out_specs=(
            pl.BlockSpec((CH, RLAT, width), lambda i: (0, 0, i)),
            pl.BlockSpec((8, width, LANES), lambda i: (0, i, 0)),
        ),
        compiler_params=params(),
        name="forward",
    )(control, from_north, from_south, forward)


def route_kernel(live_ref, values_ref, tile_ref, tile_row_ref, points_ref, weights_ref, project_ref, out_ref, rank_ref):
    live = live_ref[0]
    lane = lax.broadcasted_iota(jnp.int32, (1, LANES), 1)
    block = 256
    below = (
        lax.broadcasted_iota(jnp.int32, (block, block), 1) < lax.broadcasted_iota(jnp.int32, (block, block), 0)
    ).astype(F32).astype(BF16)
    base = jnp.zeros((1, LANES), F32)
    for part in range(ROWS // block):
        rows = slice(part * block, (part + 1) * block)
        index = part * block + lax.broadcasted_iota(jnp.int32, (block, 1), 0)
        named = ((tile_ref[rows, :] == lane) & (index < live)).astype(F32)
        before = mm(below, named.astype(BF16)) + base
        rank_ref[rows, :] = jnp.sum(named * before, axis=1, keepdims=True).astype(jnp.int32)
        base = base + jnp.sum(named, axis=0, keepdims=True)
    target = lax.broadcasted_iota(jnp.int32, (TILES, 1), 0)
    order = lax.broadcasted_iota(jnp.int32, (1, ROWS), 1)
    chosen = ((tile_row_ref[...] == target) & (order < live)).astype(F32).astype(BF16)
    group = lane // 32
    inner = lane % 32
    points = points_ref[...]
    latitude = points // CLON
    longitude = points - latitude * CLON
    cell_row = ((latitude // 8) * 1024 + longitude).astype(F32)
    level = (latitude % 8).astype(F32)
    weights = weights_ref[...]
    features = dot3(values_ref[...], project_ref[...])
    cell_rows = jnp.zeros((ROWS, LANES), F32)
    for point in range(4):
        features = jnp.where(inner == point, weights[:, point : point + 1], features)
        features = jnp.where(inner == 4 + point, level[:, point : point + 1], features)
        cell_rows = jnp.where(group == point, cell_row[:, point : point + 1], cell_rows)
    rank = jnp.broadcast_to(rank_ref[...], (ROWS, LANES))

    def deliver(masked):
        head, tail = split(masked)
        return mm(chosen, head) + mm(chosen, tail)

    out_ref[:, :LANES] = deliver(jnp.where(rank == inner, cell_rows, 0.0))
    for tile in range(8):
        lanes = slice((tile + 1) * LANES, (tile + 2) * LANES)
        out_ref[:, lanes] = deliver(jnp.where(rank == tile * 4 + group, features, 0.0))


def route(live_rows, obs_values, obs_tile, obs_points, obs_weights, jacobian, error_weight):
    project = jnp.pad((jacobian * error_weight).T, ((0, 0), (8, 8)))
    project = jnp.concatenate([project] * 4, axis=1)
    return pl.pallas_call(
        route_kernel,
        out_shape=jax.ShapeDtypeStruct((TILES, WORDS), F32),
        in_specs=[SM] + [VM] * 6,
        out_specs=VM,
        scratch_shapes=[pltpu.VMEM((ROWS, 1), jnp.int32)],
        compiler_params=params(),
        name="route",
    )(live_rows, obs_values, obs_tile, obs_tile.reshape(1, ROWS), obs_points, obs_weights, project)


def pick_table():
    pick = np.zeros((LANES, 4 * LANES), np.float32)
    for slot in range(4):
        for channel in range(CH):
            first = slot * LANES + channel * 8
            pick[slot * 32 + 8 + channel, first : first + 8] = -1.0
    return np.concatenate([pick, pick], axis=0)


def observe_kernel(
    rows_ref,
    cells_ref,
    gram_ref,
    pick_ref,
    control_ref,
    north_ref,
    south_ref,
    matrix_ref,
    coupling_ref,
    local_ref,
    to_north_ref,
    to_south_ref,
    index_ref,
    where_ref,
    mask_ref,
    columns_ref,
    values_ref,
    field_ref,
    index_semaphore,
    control_semaphore,
    *sums,
):
    index_ref[...] = rows_ref[:, :LANES].astype(jnp.int32)
    copy = pltpu.make_async_copy(index_ref, where_ref, index_semaphore)
    copy.start()
    control_copy = pltpu.make_async_copy(control_ref, local_ref, control_semaphore)
    control_copy.start()
    zero_rows = 256

    def clear(step, carry):
        for total in sums:
            total[pl.ds(pl.multiple_of(step * zero_rows, zero_rows), zero_rows), :] = jnp.zeros((zero_rows, LANES), F32)
        return carry

    lax.fori_loop(0, CELL_ROWS // zero_rows, clear, 0)
    lane_level = (lax.broadcasted_iota(jnp.int32, (1, LANES), 1) % 8).astype(F32)
    gram_head, gram_tail = split(gram_ref[...])
    gram_both = jnp.concatenate([gram_head, gram_tail], axis=0)

    def prepare(tile, carry):
        data = rows_ref[:, pl.ds(pl.multiple_of((tile + 1) * LANES, LANES), LANES)]
        values = mm(jnp.concatenate(split(data), axis=1), pick_ref[...])
        for slot in range(4):
            values_ref[tile * 4 + slot] = values[:, slot * LANES : (slot + 1) * LANES]
            for point in range(4):
                weight = data[:, slot * 32 + point : slot * 32 + point + 1]
                level = data[:, slot * 32 + 4 + point : slot * 32 + 5 + point]
                mask_ref[point, tile * 4 + slot] = jnp.where(level == lane_level, weight, 0.0)
        return carry

    lax.fori_loop(0, 8, prepare, 0)
    copy.wait()
    chunk = 16

    def move(fetch, store):
        def source(step, carry):
            for slot in range(SLOTS):
                if fetch is not None:
                    taken = fetch * chunk + step
                    interp = None
                    for point in range(4):
                        cell = where_ref[taken, point * 32 + slot]
                        term = cells_ref[pl.ds(cell, 1), :] * mask_ref[point, slot, pl.ds(taken, 1), :]
                        interp = term if interp is None else interp + term
                if store is not None:
                    given = store * chunk + step
                    column = columns_ref[slot, pl.ds(given, 1), :]
                    cells = [where_ref[given, point * 32 + slot] for point in range(4)]
                    fresh = [
                        sums[point][pl.ds(cells[point], 1), :] + mask_ref[point, slot, pl.ds(given, 1), :] * column
                        for point in range(4)
                    ]
                    for point in range(4):
                        sums[point][pl.ds(cells[point], 1), :] = fresh[point]
                if fetch is not None:
                    columns_ref[slot, pl.ds(taken, 1), :] = interp
            return carry

        lax.fori_loop(0, chunk, source, 0)

    def weigh(index):
        rows = pl.ds(pl.multiple_of(index * chunk, chunk), chunk)
        interp = columns_ref[:, rows, :].reshape(SLOTS * chunk, LANES)
        head, tail = split(interp)
        columns = mm(head, gram_head) + mm(jnp.concatenate([tail, head], axis=1), gram_both)
        columns_ref[:, rows, :] = columns.reshape(SLOTS, chunk, LANES) + values_ref[:, rows, :]

    move(0, None)
    weigh(0)

    def rounds(index, carry):
        move(index, index - 1)
        weigh(index)
        return carry

    last = TILES // chunk - 1
    lax.fori_loop(1, last + 1, rounds, 0)
    move(None, last)

    def turn(tile, carry):
        first = pl.multiple_of(tile * LANES, LANES)
        for group in range(8):
            piece = sums[0][pl.ds(group * 1024 + first, LANES), :]
            for total in sums[1:]:
                piece = piece + total[pl.ds(group * 1024 + first, LANES), :]
            field_ref[:, group * 8 : (group + 1) * 8, pl.ds(first, LANES)] = piece.T.reshape(CH, 8, LANES)
        return carry

    lax.fori_loop(0, 8, turn, 0)
    control_copy.wait()

    column = lax.broadcasted_iota(jnp.int32, (RLAT, 80), 1)
    for channel in range(CH):
        matrix = matrix_ref[channel]
        coupling = coupling_ref[channel]
        alpha_north = north_ref[channel, 2:3, 0:1] * coupling
        alpha_south = south_ref[channel, 2:3, 0:1] * coupling
        matrix = (
            matrix
            + jnp.where(column == 0, matrix[:, 64:65] * alpha_north, 0.0)
            + jnp.where(column == RLAT - 1, matrix[:, 72:73] * alpha_south, 0.0)
        )
        matrix_head, matrix_tail = split(matrix.T)
        head, tail = split(field_ref[channel])
        both = mm(jnp.concatenate([matrix_head, matrix_tail], axis=0), head)
        result = both[:80] + both[80:] + mm(matrix_head, tail)
        local_ref[channel] = local_ref[channel] + result[:RLAT, :CLON]
        to_north_ref[channel] = result[RLAT : RLAT + 8, :CLON]
        to_south_ref[channel] = result[RLAT + 8 :, :CLON]


def observe(rows, cells, gram, control, from_north, from_south, backward, coupling):
    edge = jax.ShapeDtypeStruct((CH, 8, CLON), F32)
    return pl.pallas_call(
        observe_kernel,
        out_shape=(jax.ShapeDtypeStruct((CH, RLAT, CLON), F32), edge, edge),
        in_specs=[VM] * 4 + [pl.BlockSpec(memory_space=pl.ANY)] + [VM] * 3 + [SM],
        out_specs=(VM, VM, VM),
        scratch_shapes=[
            pltpu.VMEM((TILES, LANES), jnp.int32),
            pltpu.SMEM((TILES, LANES), jnp.int32),
            pltpu.VMEM((4, SLOTS, TILES, LANES), F32),
            pltpu.VMEM((SLOTS, TILES, LANES), F32),
            pltpu.VMEM((SLOTS, TILES, LANES), F32),
            pltpu.VMEM((CH, RLAT, 1024), F32),
            pltpu.SemaphoreType.DMA,
            pltpu.SemaphoreType.DMA,
        ]
        + [pltpu.VMEM((CELL_ROWS, LANES), F32)] * ACCS,
        compiler_params=params(),
        name="observe",
    )(rows, cells, gram, jnp.asarray(pick_table(), BF16), control, from_north, from_south, backward, coupling)


def spectra_kernel(order_ref, local_ref, north_ref, south_ref, mend_ref, head_ref, tail_ref, gradient_ref, other_ref, mine_ref):
    for part, out_ref in ((0, other_ref), (1, mine_ref)):
        for half in range(2):
            pieces = []
            for place in (2 * half, 2 * half + 1):
                pair = order_ref[part * 4 + place]
                for inner in range(2):
                    channel = pair * 2 + inner
                    edges = jnp.concatenate([north_ref[channel], south_ref[channel]], axis=0)
                    piece = local_ref[channel] + dot3(mend_ref[channel], edges)
                    gradient_ref[channel] = piece
                    pieces.append(piece)
            head, tail = split(jnp.concatenate(pieces, axis=0))
            rows = 256
            both = mm(jnp.concatenate([head, tail], axis=0), head_ref[...])
            result = both[:rows] + both[rows:] + mm(head, tail_ref[...])
            out_ref[2 * half] = result[:128]
            out_ref[2 * half + 1] = result[128:]


def spectra(order, local, from_north, from_south, mend, head, tail):
    block = jax.ShapeDtypeStruct((4, 128, 2 * KEEP), F32)
    return pl.pallas_call(
        spectra_kernel,
        out_shape=(jax.ShapeDtypeStruct((CH, RLAT, CLON), F32), block, block),
        in_specs=[SM] + [VM] * 6,
        out_specs=(VM, VM, VM),
        compiler_params=params(),
        name="spectra",
    )(order, local, from_north, from_south, mend, head, tail)


def synthesis_kernel(order_ref, head_ref, tail_ref, *refs):
    pieces, out_ref = refs[:-1], refs[-1]
    for half in range(len(pieces) // 2):
        head, tail = split(jnp.concatenate([pieces[2 * half][...], pieces[2 * half + 1][...]], axis=0))
        both = mm(jnp.concatenate([head, tail], axis=0), head_ref[...])
        result = both[:256] + both[256:] + mm(head, tail_ref[...])
        for place in range(2):
            pair = order_ref[2 * half + place]
            for inner in range(2):
                first = place * 128 + inner * RLAT
                out_ref[pair * 2 + inner] = result[first : first + RLAT]


def synthesis(order, head, tail, pieces):
    return pl.pallas_call(
        synthesis_kernel,
        out_shape=jax.ShapeDtypeStruct((CH, RLAT, CLON), F32),
        in_specs=[SM] + [VM] * (2 + len(pieces)),
        out_specs=VM,
        compiler_params=params(),
        name="synthesis",
    )(order, head, tail, *pieces)


def body(
    control,
    inverse,
    coupling,
    jacobian,
    error_weight,
    response,
    obs_values,
    obs_tile,
    obs_points,
    obs_weights,
    live_rows,
):
    lon = lax.axis_index("lon")
    ring, core = lon // 2, lon % 2
    partner = [(i, i ^ 1) for i in range(8)]
    onward = [(i, (i + 2) % 8) for i in range(8)]
    back = [(i, (i - 2) % 8) for i in range(8)]

    forward, backward, edges, mend, alpha = band_matrices(inverse, coupling)
    edge = jax.ShapeDtypeStruct((CH, 8, CLON), F32)
    north, south = pl.pallas_call(
        edges_kernel,
        out_shape=(edge, edge),
        in_specs=[VM] * 3,
        out_specs=(VM, VM),
        compiler_params=params(),
        name="edges",
    )(control, edges, alpha)
    from_north, from_south = send_edges(north, south)

    routed = route(live_rows, obs_values, obs_tile, obs_points, obs_weights, jacobian, error_weight)
    rows = lax.all_to_all(routed, ("lat", "lon"), split_axis=0, concat_axis=0, tiled=True)

    state, cells = forward_diffusion(control, from_north, from_south, forward)
    gram = jnp.dot(jacobian * error_weight, jacobian.T, precision=EXACT)
    gram = jnp.repeat(jnp.repeat(gram, 8, axis=0), 8, axis=1)
    local, north, south = observe(
        rows, cells.reshape(CELL_ROWS, LANES), gram, control, from_north, from_south, backward, coupling
    )
    edge_north, edge_south = send_edges(north, south)
    lon_after, north = lax.optimization_barrier((lon, north))
    head, tail, head_t, tail_t = make_tables(lon_after)

    offsets = jnp.array([2, 1, 3, 0], jnp.int32)
    chips = (ring + offsets) % 4
    order = jnp.concatenate([chips * 2 + (1 - core), chips * 2 + core]).astype(jnp.int32)
    gradient, other, mine = spectra(order, local, edge_north, edge_south, mend, head, tail)
    pairs = mine + lax.ppermute(other, "lon", partner)
    far, near, prior, own = pairs[0], pairs[1], pairs[2], pairs[3]
    far_next = lax.ppermute(far[:64], "lon", onward)
    far_prior = lax.ppermute(far[64:], "lon", back)
    from_prior = lax.ppermute(jnp.concatenate([near[:64] + far_next, near[64:]]), "lon", onward)
    from_next = lax.ppermute(jnp.concatenate([prior[:64], prior[64:] + far_prior]), "lon", back)
    wavenumber = jnp.arange(KEEP, dtype=jnp.int32)
    factor = jnp.where(wavenumber == 0, 1.0, 2.0).astype(F32) * response / NLON
    spectrum = (own + from_prior + from_next) * jnp.concatenate([factor, factor])

    from_prior = lax.ppermute(spectrum, "lon", onward)
    from_next = lax.ppermute(spectrum, "lon", back)
    far_a = lax.ppermute(from_prior[:64], "lon", onward)
    far_b = lax.ppermute(from_next[64:], "lon", back)
    across = jnp.concatenate([far_a, far_b])
    pieces = [across, from_next, from_prior, spectrum]
    swapped = [lax.ppermute(piece, "lon", partner) for piece in pieces]
    direction = synthesis(order, head_t, tail_t, swapped + pieces)
    return (state, gradient, direction)


def solution(mesh):
    return jax.shard_map(
        body,
        mesh=mesh,
        in_specs=(
            P(None, "lat", "lon"),
            P("lat", None, None, None),
            P(),
            P(),
            P(),
            P(),
            P(("lat", "lon"), None),
            P(("lat", "lon"), None),
            P(("lat", "lon"), None),
            P(("lat", "lon"), None),
            P(("lat", "lon")),
        ),
        out_specs=(P(None, "lat", "lon"), P(None, "lat", "lon"), P(None, "lat", "lon")),
        check_vma=False,
    )
```

```python
import functools

import jax
import jax.numpy as jnp
import ml_dtypes
import numpy as np
from jax import lax
from jax.experimental import pallas as pl
from jax.experimental.pallas import tpu as pltpu
from jax.sharding import PartitionSpec as P

CH = 16
KEEP = 512
NLON = 7200
CLON = 900
RLAT = 64
HALF = 32
SLOTS = 32
TILES = 128
ROWS = 2048
LANES = 128
WORDS = LANES + SLOTS * 32
CELL_ROWS = 8 * 1024
ACCS = 4
F32 = jnp.float32
BF16 = jnp.bfloat16
EXACT = lax.Precision.HIGHEST
VM = pl.BlockSpec(memory_space=pltpu.VMEM)
SM = pl.BlockSpec(memory_space=pltpu.SMEM)


def params(mebibytes):
    return pltpu.CompilerParams(vmem_limit_bytes=mebibytes * 1024 * 1024)


def split(x):
    head = x.astype(BF16)
    return head, (x - head.astype(F32)).astype(BF16)


def mm(a, b):
    return jnp.dot(a, b, preferred_element_type=F32)


def dot3(a, b):
    a_head, a_tail = split(a)
    b_head, b_tail = split(b)
    rows = a.shape[0]
    both = mm(jnp.concatenate([a_head, a_tail], axis=0), b_head)
    return both[:rows] + both[rows:] + mm(a_head, b_tail)


def base_tables():
    longitude = np.arange(CLON)[:, None]
    wavenumber = np.arange(KEEP)[None, :]
    phase = 2.0 * np.pi * ((longitude * wavenumber) % NLON) / NLON
    table = np.concatenate([np.cos(phase), np.sin(phase)], axis=1).astype(np.float32)
    head = table.astype(ml_dtypes.bfloat16)
    tail = (table - head.astype(np.float32)).astype(ml_dtypes.bfloat16)
    return head, tail


def turn_tables():
    tile = np.arange(8)[:, None]
    wavenumber = np.arange(KEEP)[None, :]
    phase = 2.0 * np.pi * ((tile * wavenumber) % 8) / 8
    turns = np.stack([np.cos(phase), np.sin(phase)], axis=1).astype(np.float32)
    return np.concatenate([turns, np.zeros((8, 6, KEEP), np.float32)], axis=1)


def bands_kernel(
    field_ref, inverse_ref, coupling_ref, forward_ref, backward_ref, mend_ref, north_ref, south_ref
):
    def at(shape, axis):
        return lax.broadcasted_iota(jnp.int32, shape, axis)

    half = (HALF, LANES)
    upper_place = (at(half, 1) == at(half, 0)).astype(F32)
    lower_place = (at(half, 1) == at(half, 0) + HALF).astype(F32)
    full = (RLAT, LANES)
    column, row = at(full, 1), at(full, 0)
    few = (16, RLAT)
    few_column, few_row = at(few, 1), at(few, 0)
    few_place = at((16, 1), 0)
    last_row = RLAT - 1
    for channel in range(CH):
        c = coupling_ref[channel]
        blocks = jnp.concatenate(
            [
                jnp.dot(inverse_ref[0, channel], upper_place, precision=EXACT, preferred_element_type=F32),
                jnp.dot(inverse_ref[1, channel], lower_place, precision=EXACT, preferred_element_type=F32),
            ],
            axis=0,
        )
        step = blocks + c * (
            jnp.where(column == HALF, blocks[:, HALF - 1 : HALF], 0.0)
            + jnp.where(column == HALF - 1, blocks[:, HALF : HALF + 1], 0.0)
        )
        first, last = blocks[:, 0:1], blocks[:, last_row : last_row + 1]
        right = jnp.concatenate(
            [
                step + jnp.where(column == 64, c * first, 0.0) + jnp.where(column == 72, c * last, 0.0),
                step + jnp.where(column == 65, first, 0.0) + jnp.where(column == 73, last, 0.0),
            ],
            axis=1,
        )
        product = jnp.dot(step[:, :RLAT], right, precision=EXACT, preferred_element_type=F32)
        forward_ref[channel] = (
            product[:, :LANES]
            + jnp.where(column == 65, c * first, 0.0)
            + jnp.where(column == 73, c * last, 0.0)
        )
        backward_ref[channel] = (
            product[:, LANES:] + jnp.where(column == 64, first, 0.0) + jnp.where(column == 72, last, 0.0)
        )
        turned = step.T[:RLAT]
        mend_ref[channel] = c * (
            jnp.where(column == 0, turned[:, 0:1], 0.0)
            + jnp.where((column == 1) & (row == 0), 1.0, 0.0)
            + jnp.where(column == 2, turned[:, last_row : last_row + 1], 0.0)
            + jnp.where((column == 3) & (row == last_row), 1.0, 0.0)
        )
        edges = (
            jnp.where((few_row == 0) & (few_column == 0), 1.0, 0.0)
            + jnp.where(few_row == 1, step[0:1, :RLAT], 0.0)
            + jnp.where((few_row == 8) & (few_column == last_row), 1.0, 0.0)
            + jnp.where(few_row == 9, step[last_row : last_row + 1, :RLAT], 0.0)
        )
        rows = (
            dot3(edges, field_ref[channel])
            + jnp.where(few_place == 2, c * blocks[0:1, 0:1], 0.0)
            + jnp.where(few_place == 10, c * blocks[last_row : last_row + 1, last_row : last_row + 1], 0.0)
        )
        north_ref[channel] = rows[:8]
        south_ref[channel] = rows[8:]


def bands(control, inverse, coupling):
    matrix = jax.ShapeDtypeStruct((CH, RLAT, LANES), F32)
    edge = jax.ShapeDtypeStruct((CH, 8, CLON), F32)
    return pl.pallas_call(
        bands_kernel,
        out_shape=(matrix, matrix, matrix, edge, edge),
        in_specs=[VM, VM, SM],
        out_specs=(VM,) * 5,
        compiler_params=params(24),
        name="bands",
    )(control, inverse, coupling)


def send_edges(north, south):
    count = lax.axis_size("lat")
    from_south = lax.ppermute(north, "lat", [(i + 1, i) for i in range(count - 1)])
    from_north = lax.ppermute(south, "lat", [(i, i + 1) for i in range(count - 1)])
    return from_north, from_south


def forward_kernel(field_ref, north_ref, south_ref, matrix_ref, state_ref, cells_ref):
    column = lax.broadcasted_iota(jnp.int32, (RLAT, LANES), 1)
    for channel in range(CH):
        matrix = matrix_ref[channel]
        alpha_north = north_ref[channel, 2:3, 0:1]
        alpha_south = south_ref[channel, 2:3, 0:1]
        matrix = (
            matrix
            + jnp.where(column == 0, matrix[:, 65:66] * alpha_north, 0.0)
            + jnp.where(column == RLAT - 1, matrix[:, 73:74] * alpha_south, 0.0)
        )
        field = jnp.concatenate([field_ref[channel], north_ref[channel], south_ref[channel]], axis=0)
        state_ref[channel] = dot3(matrix[:, :80], field)
    for group in range(8):
        for lane_tile in range(2):
            lanes = slice(lane_tile * LANES, (lane_tile + 1) * LANES)
            piece = state_ref[:, group * 8 : (group + 1) * 8, lanes].reshape(LANES, LANES)
            cells_ref[group, lanes, :] = piece.T


def forward_diffusion(control, from_north, from_south, forward):
    width = 256
    return pl.pallas_call(
        forward_kernel,
        grid=(4,),
        out_shape=(
            jax.ShapeDtypeStruct((CH, RLAT, CLON), F32),
            jax.ShapeDtypeStruct((8, 1024, LANES), F32),
        ),
        in_specs=[
            pl.BlockSpec((CH, RLAT, width), lambda i: (0, 0, i)),
            pl.BlockSpec((CH, 8, width), lambda i: (0, 0, i)),
            pl.BlockSpec((CH, 8, width), lambda i: (0, 0, i)),
            pl.BlockSpec((CH, RLAT, LANES), lambda i: (0, 0, 0)),
        ],
        out_specs=(
            pl.BlockSpec((CH, RLAT, width), lambda i: (0, 0, i)),
            pl.BlockSpec((8, width, LANES), lambda i: (0, i, 0)),
        ),
        compiler_params=params(28),
        name="forward",
    )(control, from_north, from_south, forward)


def route_kernel(live_ref, values_ref, tile_ref, points_ref, weights_ref, project_ref, out_ref, turned_ref, column_ref, rank_ref):
    live = live_ref[0]
    lane = lax.broadcasted_iota(jnp.int32, (1, LANES), 1)
    order = lax.broadcasted_iota(jnp.int32, (1, ROWS), 1)
    points = points_ref[...]
    latitude = points // CLON
    turned_ref[0:4, :] = ((latitude // 8) * 1024 + (points - latitude * CLON)).astype(F32)
    turned_ref[4:8, :] = weights_ref[...]
    turned_ref[8:12, :] = (latitude % 8).astype(F32)
    alive = jnp.where(order < live, tile_ref[...], -1)
    turned_ref[12:13, :] = alive.astype(F32)
    for part in range(ROWS // LANES):
        some = slice(part * LANES, (part + 1) * LANES)
        column_ref[some, :] = turned_ref[:, some].T
    block = 256
    below = (
        lax.broadcasted_iota(jnp.int32, (block, block), 1) < lax.broadcasted_iota(jnp.int32, (block, block), 0)
    ).astype(F32).astype(BF16)
    lane_number = lane.astype(F32)
    base = jnp.zeros((1, LANES), F32)
    for part in range(ROWS // block):
        rows = slice(part * block, (part + 1) * block)
        named = (column_ref[rows, 12:13] == lane_number).astype(F32)
        before = mm(below, named.astype(BF16)) + base
        rank_ref[rows, :] = jnp.broadcast_to(jnp.sum(named * before, axis=1, keepdims=True), (block, LANES))
        base = base + jnp.sum(named, axis=0, keepdims=True)
    chosen = (alive == lax.broadcasted_iota(jnp.int32, (TILES, 1), 0)).astype(F32).astype(BF16)
    group = lane // 32
    inner = lane % 32
    features = dot3(values_ref[...], project_ref[...])
    cell_rows = jnp.zeros((ROWS, LANES), F32)
    for point in range(4):
        features = jnp.where(inner == point, column_ref[:, 4 + point : 5 + point], features)
        features = jnp.where(inner == 4 + point, column_ref[:, 8 + point : 9 + point], features)
        cell_rows = jnp.where(group == point, column_ref[:, point : point + 1], cell_rows)
    rank = rank_ref[...]

    def deliver(masked):
        both = mm(chosen, jnp.concatenate(split(masked), axis=1))
        return both[:, :LANES] + both[:, LANES:]

    out_ref[:, 0, :LANES] = deliver(jnp.where(rank == inner.astype(F32), cell_rows, 0.0))
    for tile in range(8):
        lanes = slice((tile + 1) * LANES, (tile + 2) * LANES)
        out_ref[:, 0, lanes] = deliver(jnp.where(rank == (tile * 4 + group).astype(F32), features, 0.0))


def route(live_rows, obs_values, obs_tile, obs_points, obs_weights, jacobian, error_weight):
    project = jnp.pad((jacobian * error_weight).T, ((0, 0), (8, 8)))
    project = jnp.concatenate([project] * 4, axis=1)
    return pl.pallas_call(
        route_kernel,
        out_shape=jax.ShapeDtypeStruct((TILES, 1, WORDS), F32),
        in_specs=[SM] + [VM] * 5,
        out_specs=VM,
        scratch_shapes=[
            pltpu.VMEM((LANES, ROWS), F32),
            pltpu.VMEM((ROWS, LANES), F32),
            pltpu.VMEM((ROWS, LANES), F32),
        ],
        compiler_params=params(32),
        name="route",
    )(live_rows, obs_values, obs_tile.T, obs_points.T, obs_weights.T, project)


def pick_table():
    pick = np.zeros((LANES, 4 * LANES), np.float32)
    for slot in range(4):
        for channel in range(CH):
            first = slot * LANES + channel * 8
            pick[slot * 32 + 8 + channel, first : first + 8] = -1.0
    return np.concatenate([pick, pick], axis=0)


def observe_kernel(
    rows_ref,
    cells_ref,
    gram_ref,
    pick_ref,
    matrix_ref,
    field_ref,
    to_north_ref,
    to_south_ref,
    index_ref,
    where_ref,
    mask_ref,
    columns_ref,
    values_ref,
    index_semaphore,
    *sums,
):
    index_ref[...] = rows_ref[:, :LANES].astype(jnp.int32)
    copy = pltpu.make_async_copy(index_ref, where_ref, index_semaphore)
    copy.start()
    zero_rows = 256

    def clear(step, carry):
        for total in sums:
            total[pl.ds(pl.multiple_of(step * zero_rows, zero_rows), zero_rows), :] = jnp.zeros((zero_rows, LANES), F32)
        return carry

    lax.fori_loop(0, CELL_ROWS // zero_rows, clear, 0)
    lane_level = (lax.broadcasted_iota(jnp.int32, (1, LANES), 1) % 8).astype(F32)
    gram_head, gram_tail = split(gram_ref[...])
    gram_both = jnp.concatenate([gram_head, gram_tail], axis=0)

    def prepare(tile, carry):
        data = rows_ref[:, pl.ds(pl.multiple_of((tile + 1) * LANES, LANES), LANES)]
        values = mm(jnp.concatenate(split(data), axis=1), pick_ref[...])
        for slot in range(4):
            values_ref[tile * 4 + slot] = values[:, slot * LANES : (slot + 1) * LANES]
            for point in range(4):
                weight = data[:, slot * 32 + point : slot * 32 + point + 1]
                level = data[:, slot * 32 + 4 + point : slot * 32 + 5 + point]
                mask_ref[point, tile * 4 + slot] = jnp.where(level == lane_level, weight, 0.0)
        return carry

    lax.fori_loop(0, 8, prepare, 0)
    copy.wait()
    chunk = 16

    def move(fetch, store):
        def source(step, carry):
            for slot in range(SLOTS):
                if fetch is not None:
                    taken = fetch * chunk + step
                    interp = None
                    for point in range(4):
                        cell = where_ref[taken, point * 32 + slot]
                        term = cells_ref[pl.ds(cell, 1), :] * mask_ref[point, slot, pl.ds(taken, 1), :]
                        interp = term if interp is None else interp + term
                if store is not None:
                    given = store * chunk + step
                    column = columns_ref[slot, pl.ds(given, 1), :]
                    cells = [where_ref[given, point * 32 + slot] for point in range(4)]
                    fresh = [
                        sums[point][pl.ds(cells[point], 1), :] + mask_ref[point, slot, pl.ds(given, 1), :] * column
                        for point in range(4)
                    ]
                    for point in range(4):
                        sums[point][pl.ds(cells[point], 1), :] = fresh[point]
                if fetch is not None:
                    columns_ref[slot, pl.ds(taken, 1), :] = interp
            return carry

        lax.fori_loop(0, chunk, source, 0)

    def weigh(index):
        rows = pl.ds(pl.multiple_of(index * chunk, chunk), chunk)
        interp = columns_ref[:, rows, :].reshape(SLOTS * chunk, LANES)
        head, tail = split(interp)
        columns = mm(head, gram_head) + mm(jnp.concatenate([tail, head], axis=1), gram_both)
        columns_ref[:, rows, :] = columns.reshape(SLOTS, chunk, LANES) + values_ref[:, rows, :]

    move(0, None)
    weigh(0)

    def rounds(index, carry):
        move(index, index - 1)
        weigh(index)
        return carry

    last = TILES // chunk - 1
    lax.fori_loop(1, last + 1, rounds, 0)
    move(None, last)

    def turn(tile, carry):
        first = pl.multiple_of(tile * LANES, LANES)
        for group in range(8):
            piece = sums[0][pl.ds(group * 1024 + first, LANES), :]
            for total in sums[1:]:
                piece = piece + total[pl.ds(group * 1024 + first, LANES), :]
            field_ref[:, group * 8 : (group + 1) * 8, pl.ds(first, LANES)] = piece.T.reshape(CH, 8, LANES)
        return carry

    lax.fori_loop(0, 8, turn, 0)

    for channel in range(CH):
        result = dot3(matrix_ref[channel].T[RLAT : RLAT + 16], field_ref[channel])
        to_north_ref[channel] = result[0:2, :CLON]
        to_south_ref[channel] = result[8:10, :CLON]


def observe(rows, cells, gram, backward):
    edge = jax.ShapeDtypeStruct((CH, 2, CLON), F32)
    return pl.pallas_call(
        observe_kernel,
        out_shape=(jax.ShapeDtypeStruct((CH, RLAT, 1024), F32), edge, edge),
        in_specs=[VM] * 5,
        out_specs=(VM, VM, VM),
        scratch_shapes=[
            pltpu.VMEM((TILES, LANES), jnp.int32),
            pltpu.SMEM((TILES, LANES), jnp.int32),
            pltpu.VMEM((4, SLOTS, TILES, LANES), F32),
            pltpu.VMEM((SLOTS, TILES, LANES), F32),
            pltpu.VMEM((SLOTS, TILES, LANES), F32),
            pltpu.SemaphoreType.DMA,
        ]
        + [pltpu.VMEM((CELL_ROWS, LANES), F32)] * ACCS,
        compiler_params=params(52),
        name="observe",
    )(rows, cells, gram, jnp.asarray(pick_table(), BF16), backward)


def adjoint_kernel(field_ref, control_ref, matrix_ref, north_ref, south_ref, coupling_ref, local_ref):
    column = lax.broadcasted_iota(jnp.int32, (RLAT, LANES), 1)
    for inner in range(4):
        matrix = matrix_ref[inner]
        coupling = coupling_ref[pl.program_id(0) * 4 + inner]
        alpha_north = north_ref[inner, 2:3, 0:1] * coupling
        alpha_south = south_ref[inner, 2:3, 0:1] * coupling
        matrix = (
            matrix
            + jnp.where(column == 0, matrix[:, 64:65] * alpha_north, 0.0)
            + jnp.where(column == RLAT - 1, matrix[:, 72:73] * alpha_south, 0.0)
        )
        local_ref[inner] = control_ref[inner] + dot3(matrix.T[:RLAT], field_ref[inner])[:, :CLON]


def adjoint_diffusion(field, control, backward, from_north, from_south, coupling):
    def four(*shape):
        return pl.BlockSpec((4,) + shape, lambda i: (i, 0, 0))

    return pl.pallas_call(
        adjoint_kernel,
        grid=(4,),
        out_shape=jax.ShapeDtypeStruct((CH, RLAT, CLON), F32),
        in_specs=[four(RLAT, 1024), four(RLAT, CLON), four(RLAT, LANES), four(8, LANES), four(8, LANES), SM],
        out_specs=four(RLAT, CLON),
        cost_estimate=pl.CostEstimate(flops=6 * 64 * 64 * 16 * 1024, bytes_accessed=12 << 20, transcendentals=0),
        compiler_params=params(20),
        name="adjoint",
    )(field, control, backward, from_north, from_south, coupling)


ANY = pl.BlockSpec(memory_space=pl.ANY)
DFT_COST = pl.CostEstimate(flops=6 * 256 * 1024 * 1024, bytes_accessed=8 << 20, transcendentals=0)


def spectra_kernel(base, added, outputs, order_ref, local_any, north_ref, south_ref, mend_ref, head_ref, tail_ref, turn_ref, *refs):
    if added:
        add_ref, refs = refs[0], refs[1:]
    gradient_any, refs = refs[0], refs[1:]
    out_refs, (field_ref, in_semaphores, out_semaphores) = refs[:outputs], refs[outputs:]
    channels = [order_ref[base + i] for i in range(4)]
    loads = [
        pltpu.make_async_copy(local_any.at[channels[i]], field_ref.at[i], in_semaphores.at[i]) for i in range(4)
    ]
    for load in loads:
        load.start()
    for load in loads:
        load.wait()
    for here, channel in enumerate(channels):
        mend = mend_ref[channel]
        north, south = north_ref[channel], south_ref[channel]
        field_ref[here] = (
            field_ref[here]
            + mend[:, 0:1] * north[0:1]
            + mend[:, 1:2] * north[1:2]
            + mend[:, 2:3] * south[0:1]
            + mend[:, 3:4] * south[1:2]
        )
    saves = [
        pltpu.make_async_copy(field_ref.at[i], gradient_any.at[channels[i]], out_semaphores.at[i]) for i in range(4)
    ]
    for save in saves:
        save.start()
    rows = 256
    head, tail = split(field_ref[...].reshape(rows, CLON))
    both = mm(jnp.concatenate([head, tail], axis=0), head_ref[...])
    result = both[:rows] + both[rows:] + mm(head, tail_ref[...])
    cos, sin = result[:, :KEEP], result[:, KEEP:]
    turn_cos, turn_sin = turn_ref[0:1, :], turn_ref[1:2, :]
    turned = (cos * turn_cos - sin * turn_sin, sin * turn_cos + cos * turn_sin)
    for part in range(2):
        lanes = slice(part * KEEP, (part + 1) * KEEP)
        for here in range(4):
            piece = turned[part][here * RLAT : (here + 1) * RLAT]
            if added:
                piece = piece + add_ref[here, :, lanes]
            out_refs[here * outputs // 4][here % (4 // outputs), :, lanes] = piece
    for save in saves:
        save.wait()


def spectra(base, order, local, north, south, mend, tables, turns, add=None):
    operands = [order, local, north, south, mend, *tables, turns]
    specs = [SM, ANY] + [VM] * 6
    outputs = 1
    if add is not None:
        operands.append(add)
        specs.append(VM)
        outputs = 2
    block = jax.ShapeDtypeStruct((4 // outputs, RLAT, 2 * KEEP), F32)
    return pl.pallas_call(
        functools.partial(spectra_kernel, base, add is not None, outputs),
        out_shape=(jax.ShapeDtypeStruct((CH, RLAT, CLON), F32),) + (block,) * outputs,
        in_specs=specs,
        out_specs=(ANY,) + (VM,) * outputs,
        scratch_shapes=[
            pltpu.VMEM((4, RLAT, CLON), F32),
            pltpu.SemaphoreType.DMA((4,)),
            pltpu.SemaphoreType.DMA((4,)),
        ],
        input_output_aliases={1: 0},
        cost_estimate=DFT_COST,
        compiler_params=params(24),
        name="spectra",
    )(*operands)


def synthesis_kernel(place, resumed, order_ref, head_ref, tail_ref, turn_ref, *refs):
    if resumed:
        refs = refs[1:]
    pieces, (out_any, field_ref, semaphores) = refs[:-3], refs[-3:]
    values = jnp.concatenate([piece[...] for piece in pieces], axis=0)
    cos, sin = values[:, :KEEP], values[:, KEEP:]
    turn_cos, turn_sin = turn_ref[0:1, :], turn_ref[1:2, :]
    values = jnp.concatenate([cos * turn_cos + sin * turn_sin, sin * turn_cos - cos * turn_sin], axis=1)
    head, tail = split(values)
    rows = 256
    both = mm(jnp.concatenate([head, tail], axis=0), head_ref[...])
    result = both[:rows] + both[rows:] + mm(head, tail_ref[...])
    field_ref[...] = result.reshape(4, RLAT, CLON)
    saves = [
        pltpu.make_async_copy(
            field_ref.at[pl.ds(2 * i, 2)], out_any.at[pl.ds(order_ref[place + 8 * (1 - i)], 2)], semaphores.at[i]
        )
        for i in range(2)
    ]
    for save in saves:
        save.start()
    for save in saves:
        save.wait()


def synthesis(place, order, tables, turns, pieces, before=None):
    operands = [order, *tables, turns]
    specs = [SM] + [VM] * 3
    if before is not None:
        operands.append(before)
        specs.append(ANY)
    return pl.pallas_call(
        functools.partial(synthesis_kernel, place, before is not None),
        out_shape=jax.ShapeDtypeStruct((CH, RLAT, CLON), F32),
        in_specs=specs + [VM] * len(pieces),
        out_specs=ANY,
        scratch_shapes=[pltpu.VMEM((4, RLAT, CLON), F32), pltpu.SemaphoreType.DMA((2,))],
        input_output_aliases={} if before is None else {4: 0},
        cost_estimate=DFT_COST,
        compiler_params=params(24),
        name="synthesis",
    )(*operands, *pieces)


def body(
    control,
    inverse,
    coupling,
    jacobian,
    error_weight,
    response,
    obs_values,
    obs_tile,
    obs_points,
    obs_weights,
    live_rows,
):
    lon = lax.axis_index("lon")
    ring, core = lon // 2, lon % 2
    partner = [(i, i ^ 1) for i in range(8)]
    onward = [(i, (i + 2) % 8) for i in range(8)]
    back = [(i, (i - 2) % 8) for i in range(8)]

    forward, backward, mend, north, south = bands(control, inverse, coupling)
    from_north, from_south = send_edges(north, south)

    routed = route(live_rows, obs_values, obs_tile, obs_points, obs_weights, jacobian, error_weight)
    rows = lax.all_to_all(routed, ("lat", "lon"), split_axis=0, concat_axis=0, tiled=True)

    state, cells = forward_diffusion(control, from_north, from_south, forward)
    gram = jnp.dot(jacobian * error_weight, jacobian.T, precision=EXACT)
    gram = jnp.repeat(jnp.repeat(gram, 8, axis=0), 8, axis=1)
    field, north, south = observe(
        rows.reshape(TILES, WORDS), cells.reshape(CELL_ROWS, LANES), gram, backward
    )
    edge_north, edge_south = send_edges(north, south)
    gradient = adjoint_diffusion(field, control, backward, from_north, from_south, coupling)

    head, tail = base_tables()
    tables = (jnp.asarray(head), jnp.asarray(tail))
    across_tables = (jnp.asarray(np.ascontiguousarray(head.T)), jnp.asarray(np.ascontiguousarray(tail.T)))
    turns = lax.dynamic_index_in_dim(jnp.asarray(turn_tables()), lon, 0, keepdims=False)
    chips = (ring + jnp.array([2, 1, 2, 3, 1, 3, 0, 0], jnp.int32)) % 4
    halves = jnp.array([0, 1, 1, 0, 0, 1, 0, 1], jnp.int32)
    order = jnp.concatenate([chips * 4 + 2 * (1 - core) + halves, chips * 4 + 2 * core + halves]).astype(jnp.int32)

    def analyse(base, gradient, add=None):
        return spectra(base, order, gradient, edge_north, edge_south, mend, tables, turns, add)

    def swap(piece):
        return lax.ppermute(piece, "lon", partner)

    gradient, ahead = analyse(0, gradient)
    ahead = swap(ahead)
    gradient, behind = analyse(4, gradient)
    behind = swap(behind)
    gradient, to_next, to_prior = analyse(8, gradient, ahead)
    from_prior = lax.ppermute(to_next, "lon", onward)
    from_next = lax.ppermute(to_prior, "lon", back)
    gradient, sides, own = analyse(12, gradient, behind)
    last_prior = lax.ppermute(sides[0] + from_prior[0], "lon", onward)
    last_next = lax.ppermute(sides[1] + from_next[0], "lon", back)
    wavenumber = jnp.arange(KEEP, dtype=jnp.int32)
    factor = jnp.where(wavenumber == 0, 1.0, 2.0).astype(F32) * response / NLON
    spectrum = jnp.concatenate(
        [own[0] + last_prior + from_next[1], own[1] + from_prior[1] + last_next]
    ) * jnp.concatenate([factor, factor])

    from_prior = lax.ppermute(spectrum, "lon", onward)
    from_next = lax.ppermute(spectrum, "lon", back)
    direction = synthesis(6, order, across_tables, turns, [spectrum, swap(spectrum)])
    from_prior, from_next, direction = lax.optimization_barrier((from_prior, from_next, direction))
    far_a = lax.ppermute(from_prior[:64], "lon", onward)
    far_b = lax.ppermute(from_next[64:], "lon", back)
    direction = synthesis(3, order, across_tables, turns, [from_prior, swap(from_prior)], direction)
    direction = synthesis(4, order, across_tables, turns, [from_next, swap(from_next)], direction)
    far_a, far_b, direction = lax.optimization_barrier((far_a, far_b, direction))
    direction = synthesis(0, order, across_tables, turns, [far_a, far_b, swap(far_a), swap(far_b)], direction)
    return (state, gradient, direction)


def solution(mesh):
    return jax.shard_map(
        body,
        mesh=mesh,
        in_specs=(
            P(None, "lat", "lon"),
            P("lat", None, None, None),
            P(),
            P(),
            P(),
            P(),
            P(("lat", "lon"), None),
            P(("lat", "lon"), None),
            P(("lat", "lon"), None),
            P(("lat", "lon"), None),
            P(("lat", "lon")),
        ),
        out_specs=(P(None, "lat", "lon"), P(None, "lat", "lon"), P(None, "lat", "lon")),
        check_vma=False,
    )
```

```python
import functools

import jax
import jax.numpy as jnp
import ml_dtypes
import numpy as np
from jax import lax
from jax.experimental import pallas as pl
from jax.experimental.pallas import tpu as pltpu
from jax.sharding import PartitionSpec as P

CH = 16
KEEP = 512
NLON = 7200
CLON = 900
RLAT = 64
HALF = 32
SLOTS = 32
TILES = 128
ROWS = 2048
LANES = 128
WORDS = LANES + SLOTS * 32
CELL_ROWS = 8 * 1024
ACCS = 4
F32 = jnp.float32
BF16 = jnp.bfloat16
EXACT = lax.Precision.HIGHEST
VM = pl.BlockSpec(memory_space=pltpu.VMEM)
SM = pl.BlockSpec(memory_space=pltpu.SMEM)


def params(mebibytes):
    return pltpu.CompilerParams(vmem_limit_bytes=mebibytes * 1024 * 1024)


def split(x):
    head = x.astype(BF16)
    return head, (x - head.astype(F32)).astype(BF16)


def mm(a, b):
    return jnp.dot(a, b, preferred_element_type=F32)


def dot3(a, b):
    a_head, a_tail = split(a)
    b_head, b_tail = split(b)
    rows = a.shape[0]
    both = mm(jnp.concatenate([a_head, a_tail], axis=0), b_head)
    return both[:rows] + both[rows:] + mm(a_head, b_tail)


def base_tables():
    longitude = np.arange(CLON)[:, None]
    wavenumber = np.arange(KEEP)[None, :]
    phase = 2.0 * np.pi * ((longitude * wavenumber) % NLON) / NLON
    table = np.concatenate([np.cos(phase), np.sin(phase)], axis=1).astype(np.float32)
    head = table.astype(ml_dtypes.bfloat16)
    tail = (table - head.astype(np.float32)).astype(ml_dtypes.bfloat16)
    return head, tail


def turn_tables():
    tile = np.arange(8)[:, None]
    wavenumber = np.arange(KEEP)[None, :]
    phase = 2.0 * np.pi * ((tile * wavenumber) % 8) / 8
    turns = np.stack([np.cos(phase), np.sin(phase)], axis=1).astype(np.float32)
    return np.concatenate([turns, np.zeros((8, 6, KEEP), np.float32)], axis=1)


def bands_kernel(
    field_ref, inverse_ref, coupling_ref, forward_ref, backward_ref, mend_ref, north_ref, south_ref
):
    def at(shape, axis):
        return lax.broadcasted_iota(jnp.int32, shape, axis)

    half = (HALF, LANES)
    upper_place = (at(half, 1) == at(half, 0)).astype(F32).astype(BF16)
    lower_place = (at(half, 1) == at(half, 0) + HALF).astype(F32).astype(BF16)

    def put(block, place):
        both = mm(jnp.concatenate(split(block), axis=0), place)
        return both[:HALF] + both[HALF:]

    full = (RLAT, LANES)
    column, row = at(full, 1), at(full, 0)
    few = (16, RLAT)
    few_column, few_row = at(few, 1), at(few, 0)
    few_place = at((16, 1), 0)
    last_row = RLAT - 1
    for channel in range(4):
        c = coupling_ref[pl.program_id(0) * 4 + channel]
        blocks = jnp.concatenate(
            [
                put(inverse_ref[0, channel], upper_place),
                put(inverse_ref[1, channel], lower_place),
            ],
            axis=0,
        )
        step = blocks + c * (
            jnp.where(column == HALF, blocks[:, HALF - 1 : HALF], 0.0)
            + jnp.where(column == HALF - 1, blocks[:, HALF : HALF + 1], 0.0)
        )
        first, last = blocks[:, 0:1], blocks[:, last_row : last_row + 1]
        right = jnp.concatenate(
            [
                step + jnp.where(column == 64, c * first, 0.0) + jnp.where(column == 72, c * last, 0.0),
                step + jnp.where(column == 65, first, 0.0) + jnp.where(column == 73, last, 0.0),
            ],
            axis=1,
        )
        product = dot3(step[:, :RLAT], right)
        forward_ref[channel] = (
            product[:, :LANES]
            + jnp.where(column == 65, c * first, 0.0)
            + jnp.where(column == 73, c * last, 0.0)
        )
        backward_ref[channel] = (
            product[:, LANES:] + jnp.where(column == 64, first, 0.0) + jnp.where(column == 72, last, 0.0)
        )
        turned = step.T[:RLAT]
        mend_ref[channel] = c * (
            jnp.where(column == 0, turned[:, 0:1], 0.0)
            + jnp.where((column == 1) & (row == 0), 1.0, 0.0)
            + jnp.where(column == 2, turned[:, last_row : last_row + 1], 0.0)
            + jnp.where((column == 3) & (row == last_row), 1.0, 0.0)
        )
        edges = (
            jnp.where((few_row == 0) & (few_column == 0), 1.0, 0.0)
            + jnp.where(few_row == 1, step[0:1, :RLAT], 0.0)
            + jnp.where((few_row == 8) & (few_column == last_row), 1.0, 0.0)
            + jnp.where(few_row == 9, step[last_row : last_row + 1, :RLAT], 0.0)
        )
        rows = (
            dot3(edges, field_ref[channel])
            + jnp.where(few_place == 2, c * blocks[0:1, 0:1], 0.0)
            + jnp.where(few_place == 10, c * blocks[last_row : last_row + 1, last_row : last_row + 1], 0.0)
        )
        north_ref[channel] = rows[:8]
        south_ref[channel] = rows[8:]


def bands(control, inverse, coupling):
    matrix = jax.ShapeDtypeStruct((CH, RLAT, LANES), F32)
    edge = jax.ShapeDtypeStruct((CH, 8, CLON), F32)
    return pl.pallas_call(
        bands_kernel,
        out_shape=(matrix, matrix, matrix, edge, edge),
        grid=(4,),
        in_specs=[
            pl.BlockSpec((4, RLAT, CLON), lambda i: (i, 0, 0)),
            pl.BlockSpec((2, 4, HALF, HALF), lambda i: (0, i, 0, 0)),
            SM,
        ],
        out_specs=tuple(
            pl.BlockSpec((4,) + shape, lambda i: (i, 0, 0)) for shape in ((RLAT, LANES),) * 3 + ((8, CLON),) * 2
        ),
        compiler_params=params(60),
        name="bands",
    )(control, inverse, coupling)


def send_edges(north, south):
    count = lax.axis_size("lat")
    from_south = lax.ppermute(north, "lat", [(i + 1, i) for i in range(count - 1)])
    from_north = lax.ppermute(south, "lat", [(i, i + 1) for i in range(count - 1)])
    return from_north, from_south


def forward_kernel(field_ref, north_ref, south_ref, matrix_ref, state_ref, cells_ref):
    column = lax.broadcasted_iota(jnp.int32, (RLAT, LANES), 1)
    for channel in range(CH):
        matrix = matrix_ref[channel]
        alpha_north = north_ref[channel, 2:3, 0:1]
        alpha_south = south_ref[channel, 2:3, 0:1]
        matrix = (
            matrix
            + jnp.where(column == 0, matrix[:, 65:66] * alpha_north, 0.0)
            + jnp.where(column == RLAT - 1, matrix[:, 73:74] * alpha_south, 0.0)
        )
        field = jnp.concatenate([field_ref[channel], north_ref[channel], south_ref[channel]], axis=0)
        state_ref[channel] = dot3(matrix[:, :80], field)
    for group in range(8):
        for lane_tile in range(2):
            lanes = slice(lane_tile * LANES, (lane_tile + 1) * LANES)
            piece = state_ref[:, group * 8 : (group + 1) * 8, lanes].reshape(LANES, LANES)
            cells_ref[group, lanes, :] = piece.T


def forward_diffusion(control, from_north, from_south, forward):
    width = 256
    return pl.pallas_call(
        forward_kernel,
        grid=(4,),
        out_shape=(
            jax.ShapeDtypeStruct((CH, RLAT, CLON), F32),
            jax.ShapeDtypeStruct((8, 1024, LANES), F32),
        ),
        in_specs=[
            pl.BlockSpec((CH, RLAT, width), lambda i: (0, 0, i)),
            pl.BlockSpec((CH, 8, width), lambda i: (0, 0, i)),
            pl.BlockSpec((CH, 8, width), lambda i: (0, 0, i)),
            pl.BlockSpec((CH, RLAT, LANES), lambda i: (0, 0, 0)),
        ],
        out_specs=(
            pl.BlockSpec((CH, RLAT, width), lambda i: (0, 0, i)),
            pl.BlockSpec((8, width, LANES), lambda i: (0, i, 0)),
        ),
        compiler_params=params(28),
        name="forward",
    )(control, from_north, from_south, forward)


def route_kernel(live_ref, values_ref, tile_ref, points_ref, weights_ref, project_ref, out_ref, turned_ref, column_ref, rank_ref):
    live = live_ref[0]
    lane = lax.broadcasted_iota(jnp.int32, (1, LANES), 1)
    order = lax.broadcasted_iota(jnp.int32, (1, ROWS), 1)
    points = points_ref[...]
    latitude = points // CLON
    turned_ref[0:4, :] = ((latitude // 8) * 1024 + (points - latitude * CLON)).astype(F32)
    turned_ref[4:8, :] = weights_ref[...]
    turned_ref[8:12, :] = (latitude % 8).astype(F32)
    alive = jnp.where(order < live, tile_ref[...], -1)
    turned_ref[12:13, :] = alive.astype(F32)
    for part in range(ROWS // LANES):
        some = slice(part * LANES, (part + 1) * LANES)
        column_ref[some, :] = turned_ref[:, some].T
    block = 256
    below = (
        lax.broadcasted_iota(jnp.int32, (block, block), 1) < lax.broadcasted_iota(jnp.int32, (block, block), 0)
    ).astype(F32).astype(BF16)
    lane_number = lane.astype(F32)
    base = jnp.zeros((1, LANES), F32)
    for part in range(ROWS // block):
        rows = slice(part * block, (part + 1) * block)
        named = (column_ref[rows, 12:13] == lane_number).astype(F32)
        before = mm(below, named.astype(BF16)) + base
        rank_ref[rows, :] = jnp.broadcast_to(jnp.sum(named * before, axis=1, keepdims=True), (block, LANES))
        base = base + jnp.sum(named, axis=0, keepdims=True)
    chosen = (alive == lax.broadcasted_iota(jnp.int32, (TILES, 1), 0)).astype(F32).astype(BF16)
    group = lane // 32
    inner = lane % 32
    features = dot3(values_ref[...], project_ref[...])
    cell_rows = jnp.zeros((ROWS, LANES), F32)
    for point in range(4):
        features = jnp.where(inner == point, column_ref[:, 4 + point : 5 + point], features)
        features = jnp.where(inner == 4 + point, column_ref[:, 8 + point : 9 + point], features)
        cell_rows = jnp.where(group == point, column_ref[:, point : point + 1], cell_rows)
    rank = rank_ref[...]

    def deliver(masked):
        both = mm(chosen, jnp.concatenate(split(masked), axis=1))
        return both[:, :LANES] + both[:, LANES:]

    out_ref[:, 0, :LANES] = deliver(jnp.where(rank == inner.astype(F32), cell_rows, 0.0))
    for tile in range(8):
        lanes = slice((tile + 1) * LANES, (tile + 2) * LANES)
        out_ref[:, 0, lanes] = deliver(jnp.where(rank == (tile * 4 + group).astype(F32), features, 0.0))


def route(live_rows, obs_values, obs_tile, obs_points, obs_weights, jacobian, error_weight):
    project = jnp.pad((jacobian * error_weight).T, ((0, 0), (8, 8)))
    project = jnp.concatenate([project] * 4, axis=1)
    return pl.pallas_call(
        route_kernel,
        out_shape=jax.ShapeDtypeStruct((TILES, 1, WORDS), F32),
        in_specs=[SM] + [VM] * 5,
        out_specs=VM,
        scratch_shapes=[
            pltpu.VMEM((LANES, ROWS), F32),
            pltpu.VMEM((ROWS, LANES), F32),
            pltpu.VMEM((ROWS, LANES), F32),
        ],
        compiler_params=params(20),
        name="route",
    )(live_rows, obs_values, obs_tile.T, obs_points.T, obs_weights.T, project)


def pick_table():
    pick = np.zeros((LANES, 4 * LANES), np.float32)
    for slot in range(4):
        for channel in range(CH):
            first = slot * LANES + channel * 8
            pick[slot * 32 + 8 + channel, first : first + 8] = -1.0
    return np.concatenate([pick, pick], axis=0)


def observe_kernel(
    rows_ref,
    cells_ref,
    gram_ref,
    pick_ref,
    matrix_ref,
    field_ref,
    to_north_ref,
    to_south_ref,
    index_ref,
    where_ref,
    mask_ref,
    got_ref,
    give_ref,
    values_ref,
    index_semaphore,
    *sums,
):
    cells_ref = cells_ref.reshape(CELL_ROWS, LANES)
    index_ref[...] = rows_ref[:, :LANES].astype(jnp.int32)
    copy = pltpu.make_async_copy(index_ref, where_ref, index_semaphore)
    copy.start()
    zero_rows = 256

    def clear(step, carry):
        for total in sums:
            total[pl.ds(pl.multiple_of(step * zero_rows, zero_rows), zero_rows), :] = jnp.zeros((zero_rows, LANES), F32)
        return carry

    lax.fori_loop(0, CELL_ROWS // zero_rows, clear, 0)
    lane_level = (lax.broadcasted_iota(jnp.int32, (1, LANES), 1) % 8).astype(F32)
    gram_head, gram_tail = split(gram_ref[...])
    gram_both = jnp.concatenate([gram_head, gram_tail], axis=0)

    def prepare(tile, carry):
        data = rows_ref[:, pl.ds(pl.multiple_of((tile + 1) * LANES, LANES), LANES)]
        values = mm(jnp.concatenate(split(data), axis=1), pick_ref[...])
        for slot in range(4):
            values_ref[tile * 4 + slot] = values[:, slot * LANES : (slot + 1) * LANES]
            for point in range(4):
                weight = data[:, slot * 32 + point : slot * 32 + point + 1]
                level = data[:, slot * 32 + 4 + point : slot * 32 + 5 + point]
                mask_ref[point, tile * 4 + slot] = jnp.where(level == lane_level, weight, 0.0)
        return carry

    lax.fori_loop(0, 8, prepare, 0)
    copy.wait()
    chunk = 16

    def move(fetch, store):
        def source(step, carry):
            for slot in range(SLOTS):
                if store is not None:
                    cells = [where_ref[store * chunk + step, point * 32 + slot] for point in range(4)]
                if fetch is not None:
                    taken = [
                        cells_ref[pl.ds(where_ref[fetch * chunk + step, point * 32 + slot], 1), :]
                        for point in range(4)
                    ]
                if store is not None:
                    fresh = [
                        sums[point][pl.ds(cells[point], 1), :] + give_ref[point, slot, pl.ds(step, 1), :]
                        for point in range(4)
                    ]
                    for point in range(4):
                        sums[point][pl.ds(cells[point], 1), :] = fresh[point]
                if fetch is not None:
                    for point in range(4):
                        got_ref[point, slot, pl.ds(step, 1), :] = taken[point]
            return carry

        lax.fori_loop(0, chunk, source, 0)

    def weigh(index):
        rows = pl.ds(pl.multiple_of(index * chunk, chunk), chunk)
        masks = [mask_ref[point, :, rows, :].reshape(SLOTS * chunk, LANES) for point in range(4)]
        got = [got_ref[point].reshape(SLOTS * chunk, LANES) for point in range(4)]
        interp = masks[0] * got[0] + masks[1] * got[1] + masks[2] * got[2] + masks[3] * got[3]
        head, tail = split(interp)
        columns = mm(head, gram_head) + mm(jnp.concatenate([tail, head], axis=1), gram_both)
        columns = columns + values_ref[:, rows, :].reshape(SLOTS * chunk, LANES)
        for point in range(4):
            give_ref[point] = (masks[point] * columns).reshape(SLOTS, chunk, LANES)

    move(0, None)
    weigh(0)

    def rounds(index, carry):
        move(index, index - 1)
        weigh(index)
        return carry

    last = TILES // chunk - 1
    lax.fori_loop(1, last + 1, rounds, 0)
    move(None, last)

    def turn(tile, carry):
        first = pl.multiple_of(tile * LANES, LANES)
        for group in range(8):
            piece = sums[0][pl.ds(group * 1024 + first, LANES), :]
            for total in sums[1:]:
                piece = piece + total[pl.ds(group * 1024 + first, LANES), :]
            field_ref[:, group * 8 : (group + 1) * 8, pl.ds(first, LANES)] = piece.T.reshape(CH, 8, LANES)
        return carry

    lax.fori_loop(0, 8, turn, 0)

    for channel in range(CH):
        result = dot3(matrix_ref[channel].T[RLAT : RLAT + 16], field_ref[channel])
        to_north_ref[channel] = result[0:2, :CLON]
        to_south_ref[channel] = result[8:10, :CLON]


def observe(rows, cells, gram, backward):
    edge = jax.ShapeDtypeStruct((CH, 2, CLON), F32)
    return pl.pallas_call(
        observe_kernel,
        out_shape=(jax.ShapeDtypeStruct((CH, RLAT, 1024), F32), edge, edge),
        in_specs=[VM] * 5,
        out_specs=(VM, VM, VM),
        scratch_shapes=[
            pltpu.VMEM((TILES, LANES), jnp.int32),
            pltpu.SMEM((TILES, LANES), jnp.int32),
            pltpu.VMEM((4, SLOTS, TILES, LANES), F32),
            pltpu.VMEM((4, SLOTS, 16, LANES), F32),
            pltpu.VMEM((4, SLOTS, 16, LANES), F32),
            pltpu.VMEM((SLOTS, TILES, LANES), F32),
            pltpu.SemaphoreType.DMA,
        ]
        + [pltpu.VMEM((CELL_ROWS, LANES), F32)] * ACCS,
        compiler_params=params(42),
        name="observe",
    )(rows, cells, gram, jnp.asarray(pick_table(), BF16), backward)


def adjoint_kernel(field_ref, control_ref, matrix_ref, north_ref, south_ref, coupling_ref, local_ref):
    column = lax.broadcasted_iota(jnp.int32, (RLAT, LANES), 1)
    for inner in range(4):
        matrix = matrix_ref[inner]
        coupling = coupling_ref[pl.program_id(0) * 4 + inner]
        alpha_north = north_ref[inner, 2:3, 0:1] * coupling
        alpha_south = south_ref[inner, 2:3, 0:1] * coupling
        matrix = (
            matrix
            + jnp.where(column == 0, matrix[:, 64:65] * alpha_north, 0.0)
            + jnp.where(column == RLAT - 1, matrix[:, 72:73] * alpha_south, 0.0)
        )
        local_ref[inner] = control_ref[inner] + dot3(matrix.T[:RLAT], field_ref[inner])[:, :CLON]


def adjoint_diffusion(field, control, backward, from_north, from_south, coupling):
    def four(*shape):
        return pl.BlockSpec((4,) + shape, lambda i: (i, 0, 0))

    return pl.pallas_call(
        adjoint_kernel,
        grid=(4,),
        out_shape=jax.ShapeDtypeStruct((CH, RLAT, CLON), F32),
        in_specs=[four(RLAT, 1024), four(RLAT, CLON), four(RLAT, LANES), four(8, LANES), four(8, LANES), SM],
        out_specs=four(RLAT, CLON),
        cost_estimate=pl.CostEstimate(flops=6 * 64 * 64 * 16 * 1024, bytes_accessed=12 << 20, transcendentals=0),
        compiler_params=params(20),
        name="adjoint",
    )(field, control, backward, from_north, from_south, coupling)


ANY = pl.BlockSpec(memory_space=pl.ANY)
DFT_COST = pl.CostEstimate(flops=6 * 256 * 1024 * 1024, bytes_accessed=8 << 20, transcendentals=0)


def spectra_kernel(base, added, outputs, order_ref, local_any, north_ref, south_ref, mend_ref, head_ref, tail_ref, turn_ref, *refs):
    if added:
        add_ref, refs = refs[0], refs[1:]
    gradient_any, refs = refs[0], refs[1:]
    out_refs, (field_ref, in_semaphores, out_semaphores) = refs[:outputs], refs[outputs:]
    channels = [order_ref[base + i] for i in range(4)]
    loads = [
        pltpu.make_async_copy(local_any.at[channels[i]], field_ref.at[i], in_semaphores.at[i]) for i in range(4)
    ]
    for load in loads:
        load.start()
    for load in loads:
        load.wait()
    for here, channel in enumerate(channels):
        mend = mend_ref[channel]
        north, south = north_ref[channel], south_ref[channel]
        field_ref[here] = (
            field_ref[here]
            + mend[:, 0:1] * north[0:1]
            + mend[:, 1:2] * north[1:2]
            + mend[:, 2:3] * south[0:1]
            + mend[:, 3:4] * south[1:2]
        )
    saves = [
        pltpu.make_async_copy(field_ref.at[i], gradient_any.at[channels[i]], out_semaphores.at[i]) for i in range(4)
    ]
    for save in saves:
        save.start()
    rows = 256
    head, tail = split(field_ref[...].reshape(rows, CLON))
    both = mm(jnp.concatenate([head, tail], axis=0), head_ref[...])
    result = both[:rows] + both[rows:] + mm(head, tail_ref[...])
    cos, sin = result[:, :KEEP], result[:, KEEP:]
    turn_cos, turn_sin = turn_ref[0:1, :], turn_ref[1:2, :]
    turned = (cos * turn_cos - sin * turn_sin, sin * turn_cos + cos * turn_sin)
    for part in range(2):
        lanes = slice(part * KEEP, (part + 1) * KEEP)
        for here in range(4):
            piece = turned[part][here * RLAT : (here + 1) * RLAT]
            if added:
                piece = piece + add_ref[here, :, lanes]
            out_refs[here * outputs // 4][here % (4 // outputs), :, lanes] = piece
    for save in saves:
        save.wait()


def spectra(base, order, local, north, south, mend, tables, turns, add=None):
    operands = [order, local, north, south, mend, *tables, turns]
    specs = [SM, ANY] + [VM] * 6
    outputs = 1
    if add is not None:
        operands.append(add)
        specs.append(VM)
        outputs = 2
    block = jax.ShapeDtypeStruct((4 // outputs, RLAT, 2 * KEEP), F32)
    return pl.pallas_call(
        functools.partial(spectra_kernel, base, add is not None, outputs),
        out_shape=(jax.ShapeDtypeStruct((CH, RLAT, CLON), F32),) + (block,) * outputs,
        in_specs=specs,
        out_specs=(ANY,) + (VM,) * outputs,
        scratch_shapes=[
            pltpu.VMEM((4, RLAT, CLON), F32),
            pltpu.SemaphoreType.DMA((4,)),
            pltpu.SemaphoreType.DMA((4,)),
        ],
        input_output_aliases={1: 0},
        cost_estimate=DFT_COST,
        compiler_params=params(24),
        name="spectra",
    )(*operands)


def synthesis_kernel(place, resumed, order_ref, head_ref, tail_ref, turn_ref, *refs):
    if resumed:
        refs = refs[1:]
    pieces, (out_any, field_ref, semaphores) = refs[:-3], refs[-3:]
    values = jnp.concatenate([piece[...] for piece in pieces], axis=0)
    cos, sin = values[:, :KEEP], values[:, KEEP:]
    turn_cos, turn_sin = turn_ref[0:1, :], turn_ref[1:2, :]
    values = jnp.concatenate([cos * turn_cos + sin * turn_sin, sin * turn_cos - cos * turn_sin], axis=1)
    head, tail = split(values)
    rows = 256
    both = mm(jnp.concatenate([head, tail], axis=0), head_ref[...])
    result = both[:rows] + both[rows:] + mm(head, tail_ref[...])
    field_ref[...] = result.reshape(4, RLAT, CLON)
    saves = [
        pltpu.make_async_copy(
            field_ref.at[pl.ds(2 * i, 2)], out_any.at[pl.ds(order_ref[place + 8 * (1 - i)], 2)], semaphores.at[i]
        )
        for i in range(2)
    ]
    for save in saves:
        save.start()
    for save in saves:
        save.wait()


def synthesis(place, order, tables, turns, pieces, before=None):
    operands = [order, *tables, turns]
    specs = [SM] + [VM] * 3
    if before is not None:
        operands.append(before)
        specs.append(ANY)
    return pl.pallas_call(
        functools.partial(synthesis_kernel, place, before is not None),
        out_shape=jax.ShapeDtypeStruct((CH, RLAT, CLON), F32),
        in_specs=specs + [VM] * len(pieces),
        out_specs=ANY,
        scratch_shapes=[pltpu.VMEM((4, RLAT, CLON), F32), pltpu.SemaphoreType.DMA((2,))],
        input_output_aliases={} if before is None else {4: 0},
        cost_estimate=DFT_COST,
        compiler_params=params(24),
        name="synthesis",
    )(*operands, *pieces)


def body(
    control,
    inverse,
    coupling,
    jacobian,
    error_weight,
    response,
    obs_values,
    obs_tile,
    obs_points,
    obs_weights,
    live_rows,
):
    lon = lax.axis_index("lon")
    ring, core = lon // 2, lon % 2
    partner = [(i, i ^ 1) for i in range(8)]
    onward = [(i, (i + 2) % 8) for i in range(8)]
    back = [(i, (i - 2) % 8) for i in range(8)]

    forward, backward, mend, north, south = bands(control, inverse, coupling)
    from_north, from_south = send_edges(north, south)

    routed = route(live_rows, obs_values, obs_tile, obs_points, obs_weights, jacobian, error_weight)
    rows = lax.all_to_all(routed, ("lat", "lon"), split_axis=0, concat_axis=0, tiled=True)

    state, cells = forward_diffusion(control, from_north, from_south, forward)
    gram = jnp.dot(jacobian * error_weight, jacobian.T, precision=EXACT)
    gram = jnp.repeat(jnp.repeat(gram, 8, axis=0), 8, axis=1)
    field, north, south = observe(
        rows.reshape(TILES, WORDS), cells, gram, backward
    )
    edge_north, edge_south = send_edges(north, south)
    gradient = adjoint_diffusion(field, control, backward, from_north, from_south, coupling)

    head, tail = base_tables()
    tables = (jnp.asarray(head), jnp.asarray(tail))
    across_tables = (jnp.asarray(np.ascontiguousarray(head.T)), jnp.asarray(np.ascontiguousarray(tail.T)))
    turns = lax.dynamic_index_in_dim(jnp.asarray(turn_tables()), lon, 0, keepdims=False)
    chips = (ring + jnp.array([2, 1, 2, 3, 1, 3, 0, 0], jnp.int32)) % 4
    halves = jnp.array([0, 1, 1, 0, 0, 1, 0, 1], jnp.int32)
    order = jnp.concatenate([chips * 4 + 2 * (1 - core) + halves, chips * 4 + 2 * core + halves]).astype(jnp.int32)

    def analyse(base, gradient, add=None):
        return spectra(base, order, gradient, edge_north, edge_south, mend, tables, turns, add)

    def swap(piece):
        return lax.ppermute(piece, "lon", partner)

    gradient, ahead = analyse(0, gradient)
    ahead = swap(ahead)
    gradient, behind = analyse(4, gradient)
    behind = swap(behind)
    gradient, to_next, to_prior = analyse(8, gradient, ahead)
    from_prior = lax.ppermute(to_next, "lon", onward)
    from_next = lax.ppermute(to_prior, "lon", back)
    gradient, sides, own = analyse(12, gradient, behind)
    last_prior = lax.ppermute(sides[0] + from_prior[0], "lon", onward)
    last_next = lax.ppermute(sides[1] + from_next[0], "lon", back)
    wavenumber = jnp.arange(KEEP, dtype=jnp.int32)
    factor = jnp.where(wavenumber == 0, 1.0, 2.0).astype(F32) * response / NLON
    spectrum = jnp.concatenate(
        [own[0] + last_prior + from_next[1], own[1] + from_prior[1] + last_next]
    ) * jnp.concatenate([factor, factor])

    from_prior = lax.ppermute(spectrum, "lon", onward)
    from_next = lax.ppermute(spectrum, "lon", back)
    direction = synthesis(6, order, across_tables, turns, [spectrum, swap(spectrum)])
    from_prior, from_next, direction = lax.optimization_barrier((from_prior, from_next, direction))
    far_a = lax.ppermute(from_prior[:64], "lon", onward)
    far_b = lax.ppermute(from_next[64:], "lon", back)
    direction = synthesis(3, order, across_tables, turns, [from_prior, swap(from_prior)], direction)
    direction = synthesis(4, order, across_tables, turns, [from_next, swap(from_next)], direction)
    far_a, far_b, direction = lax.optimization_barrier((far_a, far_b, direction))
    direction = synthesis(0, order, across_tables, turns, [far_a, far_b, swap(far_a), swap(far_b)], direction)
    return (state, gradient, direction)


def solution(mesh):
    return jax.shard_map(
        body,
        mesh=mesh,
        in_specs=(
            P(None, "lat", "lon"),
            P("lat", None, None, None),
            P(),
            P(),
            P(),
            P(),
            P(("lat", "lon"), None),
            P(("lat", "lon"), None),
            P(("lat", "lon"), None),
            P(("lat", "lon"), None),
            P(("lat", "lon")),
        ),
        out_specs=(P(None, "lat", "lon"), P(None, "lat", "lon"), P(None, "lat", "lon")),
        check_vma=False,
    )
```

```python
import functools

import jax
import jax.numpy as jnp
import ml_dtypes
import numpy as np
from jax import lax
from jax.experimental import pallas as pl
from jax.experimental.pallas import tpu as pltpu
from jax.sharding import PartitionSpec as P

CH = 16
KEEP = 512
NLON = 7200
CLON = 900
RLAT = 64
HALF = 32
SLOTS = 32
TILES = 128
ROWS = 2048
LANES = 128
WORDS = LANES + SLOTS * 32
CELL_ROWS = 8 * 1024
ACCS = 4
F32 = jnp.float32
BF16 = jnp.bfloat16
EXACT = lax.Precision.HIGHEST
VM = pl.BlockSpec(memory_space=pltpu.VMEM)
SM = pl.BlockSpec(memory_space=pltpu.SMEM)


def params(mebibytes):
    return pltpu.CompilerParams(vmem_limit_bytes=mebibytes * 1024 * 1024)


def split(x):
    head = x.astype(BF16)
    return head, (x - head.astype(F32)).astype(BF16)


def mm(a, b):
    return jnp.dot(a, b, preferred_element_type=F32)


def dot3(a, b):
    a_head, a_tail = split(a)
    b_head, b_tail = split(b)
    rows = a.shape[0]
    both = mm(jnp.concatenate([a_head, a_tail], axis=0), b_head)
    return both[:rows] + both[rows:] + mm(a_head, b_tail)


def base_tables():
    longitude = np.arange(CLON)[:, None]
    wavenumber = np.arange(KEEP)[None, :]
    phase = 2.0 * np.pi * ((longitude * wavenumber) % NLON) / NLON
    table = np.concatenate([np.cos(phase), np.sin(phase)], axis=1).astype(np.float32)
    head = table.astype(ml_dtypes.bfloat16)
    tail = (table - head.astype(np.float32)).astype(ml_dtypes.bfloat16)
    return head, tail


def turn_tables():
    tile = np.arange(8)[:, None]
    wavenumber = np.arange(KEEP)[None, :]
    phase = 2.0 * np.pi * ((tile * wavenumber) % 8) / 8
    turns = np.stack([np.cos(phase), np.sin(phase)], axis=1).astype(np.float32)
    return np.concatenate([turns, np.zeros((8, 6, KEEP), np.float32)], axis=1)


def bands_kernel(
    field_ref, inverse_ref, coupling_ref, forward_ref, backward_ref, mend_ref, north_ref, south_ref
):
    def at(shape, axis):
        return lax.broadcasted_iota(jnp.int32, shape, axis)

    half = (HALF, LANES)
    upper_place = (at(half, 1) == at(half, 0)).astype(F32).astype(BF16)
    lower_place = (at(half, 1) == at(half, 0) + HALF).astype(F32).astype(BF16)

    def put(block, place):
        both = mm(jnp.concatenate(split(block), axis=0), place)
        return both[:HALF] + both[HALF:]

    full = (RLAT, LANES)
    column, row = at(full, 1), at(full, 0)
    few_place = at((8, 1), 0)
    last_row = RLAT - 1
    for channel in range(4):
        c = coupling_ref[pl.program_id(0) * 4 + channel]
        blocks = jnp.concatenate(
            [
                put(inverse_ref[0, channel], upper_place),
                put(inverse_ref[1, channel], lower_place),
            ],
            axis=0,
        )
        step = blocks + c * (
            jnp.where(column == HALF, blocks[:, HALF - 1 : HALF], 0.0)
            + jnp.where(column == HALF - 1, blocks[:, HALF : HALF + 1], 0.0)
        )
        first, last = blocks[:, 0:1], blocks[:, last_row : last_row + 1]
        right = jnp.concatenate(
            [
                step + jnp.where(column == 64, c * first, 0.0) + jnp.where(column == 72, c * last, 0.0),
                step + jnp.where(column == 65, first, 0.0) + jnp.where(column == 73, last, 0.0),
            ],
            axis=1,
        )
        product = dot3(step[:, :RLAT], right)
        forward_ref[channel] = (
            product[:, :LANES]
            + jnp.where(column == 65, c * first, 0.0)
            + jnp.where(column == 73, c * last, 0.0)
        )
        backward_ref[channel] = (
            product[:, LANES:] + jnp.where(column == 64, first, 0.0) + jnp.where(column == 72, last, 0.0)
        )
        turned = step.T[:RLAT]
        mend_ref[channel] = c * (
            jnp.where(column == 0, turned[:, 0:1], 0.0)
            + jnp.where((column == 1) & (row == 0), 1.0, 0.0)
            + jnp.where(column == 2, turned[:, last_row : last_row + 1], 0.0)
            + jnp.where((column == 3) & (row == last_row), 1.0, 0.0)
        )
        field = field_ref[channel]
        top = jnp.sum(turned[:, 0:1] * field, axis=0, keepdims=True)
        bottom = jnp.sum(turned[:, last_row : last_row + 1] * field, axis=0, keepdims=True)
        for out_ref, edge, mixed, corner in (
            (north_ref, field[0:1], top, blocks[0:1, 0:1]),
            (south_ref, field[last_row:], bottom, blocks[last_row:, last_row : last_row + 1]),
        ):
            out_ref[channel] = jnp.where(
                few_place == 0, edge, jnp.where(few_place == 1, mixed, jnp.where(few_place == 2, c * corner, 0.0))
            )


def bands(control, inverse, coupling):
    matrix = jax.ShapeDtypeStruct((CH, RLAT, LANES), F32)
    edge = jax.ShapeDtypeStruct((CH, 8, CLON), F32)
    return pl.pallas_call(
        bands_kernel,
        out_shape=(matrix, matrix, matrix, edge, edge),
        grid=(4,),
        in_specs=[
            pl.BlockSpec((4, RLAT, CLON), lambda i: (i, 0, 0)),
            pl.BlockSpec((2, 4, HALF, HALF), lambda i: (0, i, 0, 0)),
            SM,
        ],
        out_specs=tuple(
            pl.BlockSpec((4,) + shape, lambda i: (i, 0, 0)) for shape in ((RLAT, LANES),) * 3 + ((8, CLON),) * 2
        ),
        compiler_params=params(60),
        name="bands",
    )(control, inverse, coupling)


def send_edges(north, south):
    count = lax.axis_size("lat")
    from_south = lax.ppermute(north, "lat", [(i + 1, i) for i in range(count - 1)])
    from_north = lax.ppermute(south, "lat", [(i, i + 1) for i in range(count - 1)])
    return from_north, from_south


def forward_kernel(field_ref, north_ref, south_ref, matrix_ref, state_ref, cells_ref):
    column = lax.broadcasted_iota(jnp.int32, (RLAT, LANES), 1)
    for channel in range(CH):
        matrix = matrix_ref[channel]
        alpha_north = north_ref[channel, 2:3, 0:1]
        alpha_south = south_ref[channel, 2:3, 0:1]
        matrix = (
            matrix
            + jnp.where(column == 0, matrix[:, 65:66] * alpha_north, 0.0)
            + jnp.where(column == RLAT - 1, matrix[:, 73:74] * alpha_south, 0.0)
        )
        field = jnp.concatenate([field_ref[channel], north_ref[channel], south_ref[channel]], axis=0)
        state_ref[channel] = dot3(matrix[:, :80], field)
    for group in range(8):
        for lane_tile in range(2):
            lanes = slice(lane_tile * LANES, (lane_tile + 1) * LANES)
            piece = state_ref[:, group * 8 : (group + 1) * 8, lanes].reshape(LANES, LANES)
            cells_ref[group, lanes, :] = piece.T


def forward_diffusion(control, from_north, from_south, forward):
    width = 256
    return pl.pallas_call(
        forward_kernel,
        grid=(4,),
        out_shape=(
            jax.ShapeDtypeStruct((CH, RLAT, CLON), F32),
            jax.ShapeDtypeStruct((8, 1024, LANES), F32),
        ),
        in_specs=[
            pl.BlockSpec((CH, RLAT, width), lambda i: (0, 0, i)),
            pl.BlockSpec((CH, 8, width), lambda i: (0, 0, i)),
            pl.BlockSpec((CH, 8, width), lambda i: (0, 0, i)),
            pl.BlockSpec((CH, RLAT, LANES), lambda i: (0, 0, 0)),
        ],
        out_specs=(
            pl.BlockSpec((CH, RLAT, width), lambda i: (0, 0, i)),
            pl.BlockSpec((8, width, LANES), lambda i: (0, i, 0)),
        ),
        compiler_params=params(60),
        name="forward",
    )(control, from_north, from_south, forward)


def route_kernel(live_ref, values_ref, tile_ref, points_ref, weights_ref, project_ref, out_ref, turned_ref, column_ref, rank_ref):
    live = live_ref[0]
    lane = lax.broadcasted_iota(jnp.int32, (1, LANES), 1)
    order = lax.broadcasted_iota(jnp.int32, (1, ROWS), 1)
    points = points_ref[...]
    latitude = points // CLON
    turned_ref[0:4, :] = ((latitude // 8) * 1024 + (points - latitude * CLON)).astype(F32)
    turned_ref[4:8, :] = weights_ref[...]
    turned_ref[8:12, :] = (latitude % 8).astype(F32)
    alive = jnp.where(order < live, tile_ref[...], -1)
    turned_ref[12:13, :] = alive.astype(F32)
    for part in range(ROWS // LANES):
        some = slice(part * LANES, (part + 1) * LANES)
        column_ref[some, :] = turned_ref[:, some].T
    block = 256
    below = (
        lax.broadcasted_iota(jnp.int32, (block, block), 1) < lax.broadcasted_iota(jnp.int32, (block, block), 0)
    ).astype(F32).astype(BF16)
    lane_number = lane.astype(F32)
    base = jnp.zeros((1, LANES), F32)
    for part in range(ROWS // block):
        rows = slice(part * block, (part + 1) * block)
        named = (column_ref[rows, 12:13] == lane_number).astype(F32)
        before = mm(below, named.astype(BF16)) + base
        rank_ref[rows, :] = jnp.broadcast_to(jnp.sum(named * before, axis=1, keepdims=True), (block, LANES))
        base = base + jnp.sum(named, axis=0, keepdims=True)
    chosen = (alive == lax.broadcasted_iota(jnp.int32, (TILES, 1), 0)).astype(F32).astype(BF16)
    group = lane // 32
    inner = lane % 32
    features = dot3(values_ref[...], project_ref[...])
    cell_rows = jnp.zeros((ROWS, LANES), F32)
    for point in range(4):
        features = jnp.where(inner == point, column_ref[:, 4 + point : 5 + point], features)
        features = jnp.where(inner == 4 + point, column_ref[:, 8 + point : 9 + point], features)
        cell_rows = jnp.where(group == point, column_ref[:, point : point + 1], cell_rows)
    rank = rank_ref[...]

    def deliver(masked):
        both = mm(chosen, jnp.concatenate(split(masked), axis=1))
        return both[:, :LANES] + both[:, LANES:]

    out_ref[:, 0, :LANES] = deliver(jnp.where(rank == inner.astype(F32), cell_rows, 0.0))
    for tile in range(8):
        lanes = slice((tile + 1) * LANES, (tile + 2) * LANES)
        out_ref[:, 0, lanes] = deliver(jnp.where(rank == (tile * 4 + group).astype(F32), features, 0.0))


def route(live_rows, obs_values, obs_tile, obs_points, obs_weights, jacobian, error_weight):
    project = jnp.pad((jacobian * error_weight).T, ((0, 0), (8, 8)))
    project = jnp.concatenate([project] * 4, axis=1)
    return pl.pallas_call(
        route_kernel,
        out_shape=jax.ShapeDtypeStruct((TILES, 1, WORDS), F32),
        in_specs=[SM] + [VM] * 5,
        out_specs=VM,
        scratch_shapes=[
            pltpu.VMEM((LANES, ROWS), F32),
            pltpu.VMEM((ROWS, LANES), F32),
            pltpu.VMEM((ROWS, LANES), F32),
        ],
        compiler_params=params(20),
        name="route",
    )(live_rows, obs_values, obs_tile.T, obs_points.T, obs_weights.T, project)


def pick_table():
    pick = np.zeros((LANES, 4 * LANES), np.float32)
    for slot in range(4):
        for channel in range(CH):
            first = slot * LANES + channel * 8
            pick[slot * 32 + 8 + channel, first : first + 8] = -1.0
    return np.concatenate([pick, pick], axis=0)


def observe_kernel(
    rows_ref,
    cells_hbm,
    gram_ref,
    pick_ref,
    matrix_ref,
    field_ref,
    to_north_ref,
    to_south_ref,
    index_ref,
    where_ref,
    mask_ref,
    got_ref,
    give_ref,
    values_ref,
    index_semaphore,
    cells_ref,
    cells_semaphore,
    *sums,
):
    cells_copy = pltpu.make_async_copy(cells_hbm, cells_ref, cells_semaphore)
    cells_copy.start()
    index_ref[...] = rows_ref[:, :LANES].astype(jnp.int32)
    copy = pltpu.make_async_copy(index_ref, where_ref, index_semaphore)
    copy.start()
    zero_rows = 256

    def clear(step, carry):
        for total in sums:
            total[pl.ds(pl.multiple_of(step * zero_rows, zero_rows), zero_rows), :] = jnp.zeros((zero_rows, LANES), F32)
        return carry

    lax.fori_loop(0, CELL_ROWS // zero_rows, clear, 0)
    twice_level = (lax.broadcasted_iota(jnp.int32, (1, LANES), 1) % 8).astype(F32) * 2.0
    gram_head, gram_tail = split(gram_ref[...])
    gram_both = jnp.concatenate([gram_head, gram_tail], axis=0)

    def prepare(tile, carry):
        data = rows_ref[:, pl.ds(pl.multiple_of((tile + 1) * LANES, LANES), LANES)]
        values = mm(jnp.concatenate(split(data), axis=1), pick_ref[...])
        marked = data + 2.0 * pltpu.roll(data, LANES - 4, 1)
        for slot in range(4):
            values_ref[tile * 4 + slot] = values[:, slot * LANES : (slot + 1) * LANES]
            for point in range(4):
                mask = marked[:, slot * 32 + point : slot * 32 + point + 1] - twice_level
                mask_ref[point, tile * 4 + slot] = jnp.where(jnp.abs(mask - 0.5) <= 0.5, mask, 0.0)
        return carry

    lax.fori_loop(0, 8, prepare, 0)
    copy.wait()
    cells_copy.wait()
    chunk = 16

    def move(fetch, store):
        def source(step, carry):
            for slot in range(SLOTS):
                if store is not None:
                    cells = [where_ref[store * chunk + step, point * 32 + slot] for point in range(4)]
                if fetch is not None:
                    taken = [
                        cells_ref[pl.ds(where_ref[fetch * chunk + step, point * 32 + slot], 1), :]
                        for point in range(4)
                    ]
                if store is not None:
                    fresh = [
                        sums[point][pl.ds(cells[point], 1), :] + give_ref[point, slot, pl.ds(step, 1), :]
                        for point in range(4)
                    ]
                    for point in range(4):
                        sums[point][pl.ds(cells[point], 1), :] = fresh[point]
                if fetch is not None:
                    for point in range(4):
                        got_ref[point, slot, pl.ds(step, 1), :] = taken[point]
            return carry

        lax.fori_loop(0, chunk, source, 0)

    def weigh(index):
        rows = pl.ds(pl.multiple_of(index * chunk, chunk), chunk)
        masks = [mask_ref[point, :, rows, :].reshape(SLOTS * chunk, LANES) for point in range(4)]
        got = [got_ref[point].reshape(SLOTS * chunk, LANES) for point in range(4)]
        interp = masks[0] * got[0] + masks[1] * got[1] + masks[2] * got[2] + masks[3] * got[3]
        head, tail = split(interp)
        columns = mm(head, gram_head) + mm(jnp.concatenate([tail, head], axis=1), gram_both)
        columns = columns + values_ref[:, rows, :].reshape(SLOTS * chunk, LANES)
        for point in range(4):
            give_ref[point] = (masks[point] * columns).reshape(SLOTS, chunk, LANES)

    move(0, None)
    weigh(0)

    def rounds(index, carry):
        move(index, index - 1)
        weigh(index)
        return carry

    last = TILES // chunk - 1
    lax.fori_loop(1, last + 1, rounds, 0)
    move(None, last)

    def turn(tile, carry):
        first = pl.multiple_of(tile * LANES, LANES)
        for group in range(8):
            piece = sums[0][pl.ds(group * 1024 + first, LANES), :]
            for total in sums[1:]:
                piece = piece + total[pl.ds(group * 1024 + first, LANES), :]
            field_ref[:, group * 8 : (group + 1) * 8, pl.ds(first, LANES)] = piece.T.reshape(CH, 8, LANES)
        return carry

    lax.fori_loop(0, 8, turn, 0)

    for channel in range(CH):
        result = dot3(matrix_ref[channel].T[RLAT : RLAT + 16], field_ref[channel])
        to_north_ref[channel] = result[0:2, :CLON]
        to_south_ref[channel] = result[8:10, :CLON]


def observe(rows, cells, gram, backward):
    edge = jax.ShapeDtypeStruct((CH, 2, CLON), F32)
    return pl.pallas_call(
        observe_kernel,
        out_shape=(jax.ShapeDtypeStruct((CH, RLAT, 1024), F32), edge, edge),
        in_specs=[VM, pl.BlockSpec(memory_space=pltpu.HBM), VM, VM, VM],
        out_specs=(VM, VM, VM),
        scratch_shapes=[
            pltpu.VMEM((TILES, LANES), jnp.int32),
            pltpu.SMEM((TILES, LANES), jnp.int32),
            pltpu.VMEM((4, SLOTS, TILES, LANES), F32),
            pltpu.VMEM((4, SLOTS, 16, LANES), F32),
            pltpu.VMEM((4, SLOTS, 16, LANES), F32),
            pltpu.VMEM((SLOTS, TILES, LANES), F32),
            pltpu.SemaphoreType.DMA,
            pltpu.VMEM((CELL_ROWS, LANES), F32),
            pltpu.SemaphoreType.DMA,
        ]
        + [pltpu.VMEM((CELL_ROWS, LANES), F32)] * ACCS,
        compiler_params=params(46),
        name="observe",
    )(rows, cells, gram, jnp.asarray(pick_table(), BF16), backward)


def adjoint_kernel(field_ref, control_ref, matrix_ref, north_ref, south_ref, coupling_ref, local_ref):
    column = lax.broadcasted_iota(jnp.int32, (RLAT, LANES), 1)
    for inner in range(4):
        matrix = matrix_ref[inner]
        coupling = coupling_ref[pl.program_id(0) * 4 + inner]
        alpha_north = north_ref[inner, 2:3, 0:1] * coupling
        alpha_south = south_ref[inner, 2:3, 0:1] * coupling
        matrix = (
            matrix
            + jnp.where(column == 0, matrix[:, 64:65] * alpha_north, 0.0)
            + jnp.where(column == RLAT - 1, matrix[:, 72:73] * alpha_south, 0.0)
        )
        local_ref[inner] = control_ref[inner] + dot3(matrix.T[:RLAT], field_ref[inner])[:, :CLON]


def adjoint_diffusion(field, control, backward, from_north, from_south, coupling):
    def four(*shape):
        return pl.BlockSpec((4,) + shape, lambda i: (i, 0, 0))

    return pl.pallas_call(
        adjoint_kernel,
        grid=(4,),
        out_shape=jax.ShapeDtypeStruct((CH, RLAT, CLON), F32),
        in_specs=[four(RLAT, 1024), four(RLAT, CLON), four(RLAT, LANES), four(8, LANES), four(8, LANES), SM],
        out_specs=four(RLAT, CLON),
        cost_estimate=pl.CostEstimate(flops=6 * 64 * 64 * 16 * 1024, bytes_accessed=12 << 20, transcendentals=0),
        compiler_params=params(20),
        name="adjoint",
    )(field, control, backward, from_north, from_south, coupling)


ANY = pl.BlockSpec(memory_space=pl.ANY)
DFT_COST = pl.CostEstimate(flops=6 * 256 * 1024 * 1024, bytes_accessed=8 << 20, transcendentals=0)


def spectra_kernel(base, added, outputs, order_ref, local_any, north_ref, south_ref, mend_ref, head_ref, tail_ref, turn_ref, *refs):
    if added:
        add_ref, refs = refs[0], refs[1:]
    gradient_any, refs = refs[0], refs[1:]
    out_refs, (field_ref, in_semaphores, out_semaphores) = refs[:outputs], refs[outputs:]
    channels = [order_ref[base + i] for i in range(4)]
    loads = [
        pltpu.make_async_copy(local_any.at[channels[i]], field_ref.at[i], in_semaphores.at[i]) for i in range(4)
    ]
    for load in loads:
        load.start()
    for load in loads:
        load.wait()
    for here, channel in enumerate(channels):
        mend = mend_ref[channel]
        north, south = north_ref[channel], south_ref[channel]
        field_ref[here] = (
            field_ref[here]
            + mend[:, 0:1] * north[0:1]
            + mend[:, 1:2] * north[1:2]
            + mend[:, 2:3] * south[0:1]
            + mend[:, 3:4] * south[1:2]
        )
    saves = [
        pltpu.make_async_copy(field_ref.at[i], gradient_any.at[channels[i]], out_semaphores.at[i]) for i in range(4)
    ]
    for save in saves:
        save.start()
    rows = 256
    head, tail = split(field_ref[...].reshape(rows, CLON))
    both = mm(jnp.concatenate([head, tail], axis=0), head_ref[...])
    result = both[:rows] + both[rows:] + mm(head, tail_ref[...])
    cos, sin = result[:, :KEEP], result[:, KEEP:]
    turn_cos, turn_sin = turn_ref[0:1, :], turn_ref[1:2, :]
    turned = (cos * turn_cos - sin * turn_sin, sin * turn_cos + cos * turn_sin)
    for part in range(2):
        lanes = slice(part * KEEP, (part + 1) * KEEP)
        for here in range(4):
            piece = turned[part][here * RLAT : (here + 1) * RLAT]
            if added:
                piece = piece + add_ref[here, :, lanes]
            out_refs[here * outputs // 4][here % (4 // outputs), :, lanes] = piece
    for save in saves:
        save.wait()


def spectra(base, order, local, north, south, mend, tables, turns, add=None):
    operands = [order, local, north, south, mend, *tables, turns]
    specs = [SM, ANY] + [VM] * 6
    outputs = 1
    if add is not None:
        operands.append(add)
        specs.append(VM)
        outputs = 2
    block = jax.ShapeDtypeStruct((4 // outputs, RLAT, 2 * KEEP), F32)
    return pl.pallas_call(
        functools.partial(spectra_kernel, base, add is not None, outputs),
        out_shape=(jax.ShapeDtypeStruct((CH, RLAT, CLON), F32),) + (block,) * outputs,
        in_specs=specs,
        out_specs=(ANY,) + (VM,) * outputs,
        scratch_shapes=[
            pltpu.VMEM((4, RLAT, CLON), F32),
            pltpu.SemaphoreType.DMA((4,)),
            pltpu.SemaphoreType.DMA((4,)),
        ],
        input_output_aliases={1: 0},
        cost_estimate=DFT_COST,
        compiler_params=params(24),
        name="spectra",
    )(*operands)


def synthesis_kernel(place, resumed, order_ref, head_ref, tail_ref, turn_ref, *refs):
    if resumed:
        refs = refs[1:]
    pieces, (out_any, field_ref, semaphores) = refs[:-3], refs[-3:]
    values = jnp.concatenate([piece[...] for piece in pieces], axis=0)
    cos, sin = values[:, :KEEP], values[:, KEEP:]
    turn_cos, turn_sin = turn_ref[0:1, :], turn_ref[1:2, :]
    values = jnp.concatenate([cos * turn_cos + sin * turn_sin, sin * turn_cos - cos * turn_sin], axis=1)
    head, tail = split(values)
    rows = 256
    both = mm(jnp.concatenate([head, tail], axis=0), head_ref[...])
    result = both[:rows] + both[rows:] + mm(head, tail_ref[...])
    field_ref[...] = result.reshape(4, RLAT, CLON)
    saves = [
        pltpu.make_async_copy(
            field_ref.at[pl.ds(2 * i, 2)], out_any.at[pl.ds(order_ref[place + 8 * (1 - i)], 2)], semaphores.at[i]
        )
        for i in range(2)
    ]
    for save in saves:
        save.start()
    for save in saves:
        save.wait()


def synthesis(place, order, tables, turns, pieces, before=None):
    operands = [order, *tables, turns]
    specs = [SM] + [VM] * 3
    if before is not None:
        operands.append(before)
        specs.append(ANY)
    return pl.pallas_call(
        functools.partial(synthesis_kernel, place, before is not None),
        out_shape=jax.ShapeDtypeStruct((CH, RLAT, CLON), F32),
        in_specs=specs + [VM] * len(pieces),
        out_specs=ANY,
        scratch_shapes=[pltpu.VMEM((4, RLAT, CLON), F32), pltpu.SemaphoreType.DMA((2,))],
        input_output_aliases={} if before is None else {4: 0},
        cost_estimate=DFT_COST,
        compiler_params=params(24),
        name="synthesis",
    )(*operands, *pieces)


def body(
    control,
    inverse,
    coupling,
    jacobian,
    error_weight,
    response,
    obs_values,
    obs_tile,
    obs_points,
    obs_weights,
    live_rows,
):
    lon = lax.axis_index("lon")
    ring, core = lon // 2, lon % 2
    partner = [(i, i ^ 1) for i in range(8)]
    onward = [(i, (i + 2) % 8) for i in range(8)]
    back = [(i, (i - 2) % 8) for i in range(8)]

    forward, backward, mend, north, south = bands(control, inverse, coupling)
    from_north, from_south = send_edges(north, south)

    routed = route(live_rows, obs_values, obs_tile, obs_points, obs_weights, jacobian, error_weight)
    rows = lax.all_to_all(routed, ("lat", "lon"), split_axis=0, concat_axis=0, tiled=True)

    state, cells = forward_diffusion(control, from_north, from_south, forward)
    gram = jnp.dot(jacobian * error_weight, jacobian.T, precision=EXACT)
    gram = jnp.repeat(jnp.repeat(gram, 8, axis=0), 8, axis=1)
    field, north, south = observe(
        rows.reshape(TILES, WORDS), cells.reshape(CELL_ROWS, LANES), gram, backward
    )
    edge_north, edge_south = send_edges(north, south)
    gradient = adjoint_diffusion(field, control, backward, from_north, from_south, coupling)

    head, tail = base_tables()
    tables = (jnp.asarray(head), jnp.asarray(tail))
    across_tables = (jnp.asarray(np.ascontiguousarray(head.T)), jnp.asarray(np.ascontiguousarray(tail.T)))
    turns = lax.dynamic_index_in_dim(jnp.asarray(turn_tables()), lon, 0, keepdims=False)
    chips = (ring + jnp.array([2, 1, 2, 3, 1, 3, 0, 0], jnp.int32)) % 4
    halves = jnp.array([0, 1, 1, 0, 0, 1, 0, 1], jnp.int32)
    order = jnp.concatenate([chips * 4 + 2 * (1 - core) + halves, chips * 4 + 2 * core + halves]).astype(jnp.int32)

    def analyse(base, gradient, add=None):
        return spectra(base, order, gradient, edge_north, edge_south, mend, tables, turns, add)

    def swap(piece):
        return lax.ppermute(piece, "lon", partner)

    gradient, ahead = analyse(0, gradient)
    ahead = swap(ahead)
    gradient, behind = analyse(4, gradient)
    behind = swap(behind)
    gradient, to_next, to_prior = analyse(8, gradient, ahead)
    from_prior = lax.ppermute(to_next, "lon", onward)
    from_next = lax.ppermute(to_prior, "lon", back)
    gradient, sides, own = analyse(12, gradient, behind)
    last_prior = lax.ppermute(sides[0] + from_prior[0], "lon", onward)
    last_next = lax.ppermute(sides[1] + from_next[0], "lon", back)
    wavenumber = jnp.arange(KEEP, dtype=jnp.int32)
    factor = jnp.where(wavenumber == 0, 1.0, 2.0).astype(F32) * response / NLON
    spectrum = jnp.concatenate(
        [own[0] + last_prior + from_next[1], own[1] + from_prior[1] + last_next]
    ) * jnp.concatenate([factor, factor])

    from_prior = lax.ppermute(spectrum, "lon", onward)
    from_next = lax.ppermute(spectrum, "lon", back)
    direction = synthesis(6, order, across_tables, turns, [spectrum, swap(spectrum)])
    from_prior, from_next, direction = lax.optimization_barrier((from_prior, from_next, direction))
    far_a = lax.ppermute(from_prior[:64], "lon", onward)
    far_b = lax.ppermute(from_next[64:], "lon", back)
    direction = synthesis(3, order, across_tables, turns, [from_prior, swap(from_prior)], direction)
    direction = synthesis(4, order, across_tables, turns, [from_next, swap(from_next)], direction)
    far_a, far_b, direction = lax.optimization_barrier((far_a, far_b, direction))
    direction = synthesis(0, order, across_tables, turns, [far_a, far_b, swap(far_a), swap(far_b)], direction)
    return (state, gradient, direction)


def solution(mesh):
    return jax.shard_map(
        body,
        mesh=mesh,
        in_specs=(
            P(None, "lat", "lon"),
            P("lat", None, None, None),
            P(),
            P(),
            P(),
            P(),
            P(("lat", "lon"), None),
            P(("lat", "lon"), None),
            P(("lat", "lon"), None),
            P(("lat", "lon"), None),
            P(("lat", "lon")),
        ),
        out_specs=(P(None, "lat", "lon"), P(None, "lat", "lon"), P(None, "lat", "lon")),
        check_vma=False,
    )
```

```python
import functools

import jax
import jax.numpy as jnp
import ml_dtypes
import numpy as np
from jax import lax
from jax.experimental import pallas as pl
from jax.experimental.pallas import tpu as pltpu
from jax.sharding import PartitionSpec as P

CH = 16
KEEP = 512
NLON = 7200
CLON = 900
RLAT = 64
HALF = 32
SLOTS = 32
TILES = 128
ROWS = 2048
LANES = 128
WORDS = LANES + SLOTS * 32
CELL_ROWS = 8 * 1024
ACCS = 4
F32 = jnp.float32
BF16 = jnp.bfloat16
EXACT = lax.Precision.HIGHEST
VM = pl.BlockSpec(memory_space=pltpu.VMEM)
SM = pl.BlockSpec(memory_space=pltpu.SMEM)


def params(mebibytes):
    return pltpu.CompilerParams(vmem_limit_bytes=mebibytes * 1024 * 1024)


def split(x):
    head = x.astype(BF16)
    return head, (x - head.astype(F32)).astype(BF16)


def mm(a, b):
    return jnp.dot(a, b, preferred_element_type=F32)


def dot3(a, b):
    a_head, a_tail = split(a)
    b_head, b_tail = split(b)
    rows = a.shape[0]
    both = mm(jnp.concatenate([a_head, a_tail], axis=0), b_head)
    return both[:rows] + both[rows:] + mm(a_head, b_tail)


def base_tables():
    longitude = np.arange(CLON)[:, None]
    wavenumber = np.arange(KEEP)[None, :]
    phase = 2.0 * np.pi * ((longitude * wavenumber) % NLON) / NLON
    table = np.concatenate([np.cos(phase), np.sin(phase)], axis=1).astype(np.float32)
    head = table.astype(ml_dtypes.bfloat16)
    tail = (table - head.astype(np.float32)).astype(ml_dtypes.bfloat16)
    return head, tail


def turn_tables():
    tile = np.arange(8)[:, None]
    wavenumber = np.arange(KEEP)[None, :]
    phase = 2.0 * np.pi * ((tile * wavenumber) % 8) / 8
    turns = np.stack([np.cos(phase), np.sin(phase)], axis=1).astype(np.float32)
    return np.concatenate([turns, np.zeros((8, 6, KEEP), np.float32)], axis=1)


def bands_kernel(
    field_ref, inverse_ref, coupling_ref, forward_ref, backward_ref, mend_ref, north_ref, south_ref
):
    def at(shape, axis):
        return lax.broadcasted_iota(jnp.int32, shape, axis)

    half = (HALF, LANES)
    upper_place = (at(half, 1) == at(half, 0)).astype(F32).astype(BF16)
    lower_place = (at(half, 1) == at(half, 0) + HALF).astype(F32).astype(BF16)

    def put(block, place):
        both = mm(jnp.concatenate(split(block), axis=0), place)
        return both[:HALF] + both[HALF:]

    full = (RLAT, LANES)
    column, row = at(full, 1), at(full, 0)
    few_place = at((8, 1), 0)
    last_row = RLAT - 1
    for channel in range(4):
        c = coupling_ref[pl.program_id(0) * 4 + channel]
        blocks = jnp.concatenate(
            [
                put(inverse_ref[0, channel], upper_place),
                put(inverse_ref[1, channel], lower_place),
            ],
            axis=0,
        )
        step = blocks + c * (
            jnp.where(column == HALF, blocks[:, HALF - 1 : HALF], 0.0)
            + jnp.where(column == HALF - 1, blocks[:, HALF : HALF + 1], 0.0)
        )
        first, last = blocks[:, 0:1], blocks[:, last_row : last_row + 1]
        right = jnp.concatenate(
            [
                step + jnp.where(column == 64, c * first, 0.0) + jnp.where(column == 72, c * last, 0.0),
                step + jnp.where(column == 65, first, 0.0) + jnp.where(column == 73, last, 0.0),
            ],
            axis=1,
        )
        product = dot3(step[:, :RLAT], right)
        forward_ref[channel] = (
            product[:, :LANES]
            + jnp.where(column == 65, c * first, 0.0)
            + jnp.where(column == 73, c * last, 0.0)
        )
        backward_ref[channel] = (
            product[:, LANES:] + jnp.where(column == 64, first, 0.0) + jnp.where(column == 72, last, 0.0)
        )
        turned = step.T[:RLAT]
        mend_ref[channel] = c * (
            jnp.where(column == 0, turned[:, 0:1], 0.0)
            + jnp.where((column == 1) & (row == 0), 1.0, 0.0)
            + jnp.where(column == 2, turned[:, last_row : last_row + 1], 0.0)
            + jnp.where((column == 3) & (row == last_row), 1.0, 0.0)
        )
        field = field_ref[channel]
        top = jnp.sum(turned[:, 0:1] * field, axis=0, keepdims=True)
        bottom = jnp.sum(turned[:, last_row : last_row + 1] * field, axis=0, keepdims=True)
        for out_ref, edge, mixed, corner in (
            (north_ref, field[0:1], top, blocks[0:1, 0:1]),
            (south_ref, field[last_row:], bottom, blocks[last_row:, last_row : last_row + 1]),
        ):
            out_ref[channel] = jnp.where(
                few_place == 0, edge, jnp.where(few_place == 1, mixed, jnp.where(few_place == 2, c * corner, 0.0))
            )


def bands(control, inverse, coupling):
    matrix = jax.ShapeDtypeStruct((CH, RLAT, LANES), F32)
    edge = jax.ShapeDtypeStruct((CH, 8, CLON), F32)
    return pl.pallas_call(
        bands_kernel,
        out_shape=(matrix, matrix, matrix, edge, edge),
        grid=(4,),
        in_specs=[
            pl.BlockSpec((4, RLAT, CLON), lambda i: (i, 0, 0)),
            pl.BlockSpec((2, 4, HALF, HALF), lambda i: (0, i, 0, 0)),
            SM,
        ],
        out_specs=tuple(
            pl.BlockSpec((4,) + shape, lambda i: (i, 0, 0)) for shape in ((RLAT, LANES),) * 3 + ((8, CLON),) * 2
        ),
        compiler_params=params(60),
        name="bands",
    )(control, inverse, coupling)


def send_edges(north, south):
    count = lax.axis_size("lat")
    from_south = lax.ppermute(north, "lat", [(i + 1, i) for i in range(count - 1)])
    from_north = lax.ppermute(south, "lat", [(i, i + 1) for i in range(count - 1)])
    return from_north, from_south


def forward_kernel(field_ref, north_ref, south_ref, matrix_ref, state_ref, cells_ref):
    column = lax.broadcasted_iota(jnp.int32, (RLAT, LANES), 1)
    for channel in range(CH):
        matrix = matrix_ref[channel]
        alpha_north = north_ref[channel, 2:3, 0:1]
        alpha_south = south_ref[channel, 2:3, 0:1]
        matrix = (
            matrix
            + jnp.where(column == 0, matrix[:, 65:66] * alpha_north, 0.0)
            + jnp.where(column == RLAT - 1, matrix[:, 73:74] * alpha_south, 0.0)
        )
        field = jnp.concatenate([field_ref[channel], north_ref[channel], south_ref[channel]], axis=0)
        state_ref[channel] = dot3(matrix[:, :80], field)
    for group in range(8):
        for lane_tile in range(2):
            lanes = slice(lane_tile * LANES, (lane_tile + 1) * LANES)
            piece = state_ref[:, group * 8 : (group + 1) * 8, lanes].reshape(LANES, LANES)
            cells_ref[group, lanes, :] = piece.T


def forward_diffusion(control, from_north, from_south, forward):
    width = 256
    return pl.pallas_call(
        forward_kernel,
        grid=(4,),
        out_shape=(
            jax.ShapeDtypeStruct((CH, RLAT, CLON), F32),
            jax.ShapeDtypeStruct((8, 1024, LANES), F32),
        ),
        in_specs=[
            pl.BlockSpec((CH, RLAT, width), lambda i: (0, 0, i)),
            pl.BlockSpec((CH, 8, width), lambda i: (0, 0, i)),
            pl.BlockSpec((CH, 8, width), lambda i: (0, 0, i)),
            pl.BlockSpec((CH, RLAT, LANES), lambda i: (0, 0, 0)),
        ],
        out_specs=(
            pl.BlockSpec((CH, RLAT, width), lambda i: (0, 0, i)),
            pl.BlockSpec((8, width, LANES), lambda i: (0, i, 0)),
        ),
        compiler_params=params(60),
        name="forward",
    )(control, from_north, from_south, forward)


def route_kernel(live_ref, values_ref, tile_ref, points_ref, weights_ref, project_ref, out_ref, turned_ref, column_ref, rank_ref):
    live = live_ref[0]
    lane = lax.broadcasted_iota(jnp.int32, (1, LANES), 1)
    order = lax.broadcasted_iota(jnp.int32, (1, ROWS), 1)
    points = points_ref[...]
    latitude = points // CLON
    turned_ref[0:4, :] = ((latitude // 8) * 1024 + (points - latitude * CLON)).astype(F32)
    turned_ref[4:8, :] = weights_ref[...]
    turned_ref[8:12, :] = (latitude % 8).astype(F32)
    alive = jnp.where(order < live, tile_ref[...], -1)
    turned_ref[12:13, :] = alive.astype(F32)
    for part in range(ROWS // LANES):
        some = slice(part * LANES, (part + 1) * LANES)
        column_ref[some, :] = turned_ref[:, some].T
    block = 256
    below = (
        lax.broadcasted_iota(jnp.int32, (block, block), 1) < lax.broadcasted_iota(jnp.int32, (block, block), 0)
    ).astype(F32).astype(BF16)
    lane_number = lane.astype(F32)
    base = jnp.zeros((1, LANES), F32)
    for part in range(ROWS // block):
        rows = slice(part * block, (part + 1) * block)
        named = (column_ref[rows, 12:13] == lane_number).astype(F32)
        before = mm(below, named.astype(BF16)) + base
        rank_ref[rows, :] = jnp.broadcast_to(jnp.sum(named * before, axis=1, keepdims=True), (block, LANES))
        base = base + jnp.sum(named, axis=0, keepdims=True)
    chosen = (alive == lax.broadcasted_iota(jnp.int32, (TILES, 1), 0)).astype(F32).astype(BF16)
    group = lane // 32
    inner = lane % 32
    features = dot3(values_ref[...], project_ref[...])
    cell_rows = jnp.zeros((ROWS, LANES), F32)
    for point in range(4):
        features = jnp.where(inner == point, column_ref[:, 4 + point : 5 + point], features)
        features = jnp.where(inner == 4 + point, column_ref[:, 8 + point : 9 + point], features)
        cell_rows = jnp.where(group == point, column_ref[:, point : point + 1], cell_rows)
    rank = rank_ref[...]

    def deliver(masked):
        both = mm(chosen, jnp.concatenate(split(masked), axis=1))
        return both[:, :LANES] + both[:, LANES:]

    out_ref[:, 0, :LANES] = deliver(jnp.where(rank == inner.astype(F32), cell_rows, 0.0))
    for tile in range(8):
        lanes = slice((tile + 1) * LANES, (tile + 2) * LANES)
        out_ref[:, 0, lanes] = deliver(jnp.where(rank == (tile * 4 + group).astype(F32), features, 0.0))


def route(live_rows, obs_values, obs_tile, obs_points, obs_weights, jacobian, error_weight):
    project = jnp.pad((jacobian * error_weight).T, ((0, 0), (8, 8)))
    project = jnp.concatenate([project] * 4, axis=1)
    return pl.pallas_call(
        route_kernel,
        out_shape=jax.ShapeDtypeStruct((TILES, 1, WORDS), F32),
        in_specs=[SM] + [VM] * 5,
        out_specs=VM,
        scratch_shapes=[
            pltpu.VMEM((LANES, ROWS), F32),
            pltpu.VMEM((ROWS, LANES), F32),
            pltpu.VMEM((ROWS, LANES), F32),
        ],
        compiler_params=params(20),
        name="route",
    )(live_rows, obs_values, obs_tile.T, obs_points.T, obs_weights.T, project)


def pick_table():
    pick = np.zeros((LANES, 4 * LANES), np.float32)
    for slot in range(4):
        for channel in range(CH):
            first = slot * LANES + channel * 8
            pick[slot * 32 + 8 + channel, first : first + 8] = -1.0
    return np.concatenate([pick, pick], axis=0)


def observe_kernel(
    rows_ref,
    cells_hbm,
    gram_ref,
    pick_ref,
    matrix_ref,
    field_ref,
    to_north_ref,
    to_south_ref,
    index_ref,
    where_ref,
    mask_ref,
    got_ref,
    give_ref,
    values_ref,
    index_semaphore,
    cells_ref,
    cells_semaphore,
    *sums,
):
    cells_copy = pltpu.make_async_copy(cells_hbm, cells_ref, cells_semaphore)
    cells_copy.start()
    index_ref[...] = rows_ref[:, :LANES].astype(jnp.int32)
    copy = pltpu.make_async_copy(index_ref, where_ref, index_semaphore)
    copy.start()
    zero_rows = 256

    def clear(step, carry):
        for total in sums:
            total[pl.ds(pl.multiple_of(step * zero_rows, zero_rows), zero_rows), :] = jnp.zeros((zero_rows, LANES), F32)
        return carry

    lax.fori_loop(0, CELL_ROWS // zero_rows, clear, 0)
    twice_level = (lax.broadcasted_iota(jnp.int32, (1, LANES), 1) % 8).astype(F32) * 2.0
    gram_head, gram_tail = split(gram_ref[...])
    gram_both = jnp.concatenate([gram_head, gram_tail], axis=0)

    def prepare(tile, carry):
        data = rows_ref[:, pl.ds(pl.multiple_of((tile + 1) * LANES, LANES), LANES)]
        values = mm(jnp.concatenate(split(data), axis=1), pick_ref[...])
        marked = data + 2.0 * pltpu.roll(data, LANES - 4, 1)
        for slot in range(4):
            values_ref[tile * 4 + slot] = values[:, slot * LANES : (slot + 1) * LANES]
            for point in range(4):
                mask = marked[:, slot * 32 + point : slot * 32 + point + 1] - twice_level
                mask_ref[point, tile * 4 + slot] = jnp.where(jnp.abs(mask - 0.5) <= 0.5, mask, 0.0)
        return carry

    lax.fori_loop(0, 8, prepare, 0)
    copy.wait()
    cells_copy.wait()
    chunk = 16

    def move(fetch, store):
        def source(step, carry):
            for slot in range(SLOTS):
                if store is not None:
                    cells = [where_ref[store * chunk + step, point * 32 + slot] for point in range(4)]
                if fetch is not None:
                    taken = [
                        cells_ref[pl.ds(where_ref[fetch * chunk + step, point * 32 + slot], 1), :]
                        for point in range(4)
                    ]
                if store is not None:
                    fresh = [
                        sums[point][pl.ds(cells[point], 1), :] + give_ref[point, slot, pl.ds(step, 1), :]
                        for point in range(4)
                    ]
                    for point in range(4):
                        sums[point][pl.ds(cells[point], 1), :] = fresh[point]
                if fetch is not None:
                    for point in range(4):
                        got_ref[point, slot, pl.ds(step, 1), :] = taken[point]
            return carry

        lax.fori_loop(0, chunk, source, 0)

    def weigh(index):
        rows = pl.ds(pl.multiple_of(index * chunk, chunk), chunk)
        masks = [mask_ref[point, :, rows, :].reshape(SLOTS * chunk, LANES) for point in range(4)]
        got = [got_ref[point].reshape(SLOTS * chunk, LANES) for point in range(4)]
        interp = masks[0] * got[0] + masks[1] * got[1] + masks[2] * got[2] + masks[3] * got[3]
        head, tail = split(interp)
        columns = mm(head, gram_head) + mm(jnp.concatenate([tail, head], axis=1), gram_both)
        columns = columns + values_ref[:, rows, :].reshape(SLOTS * chunk, LANES)
        for point in range(4):
            give_ref[point] = (masks[point] * columns).reshape(SLOTS, chunk, LANES)

    move(0, None)
    weigh(0)

    def rounds(index, carry):
        move(index, index - 1)
        weigh(index)
        return carry

    last = TILES // chunk - 1
    lax.fori_loop(1, last + 1, rounds, 0)
    move(None, last)

    def turn(tile, carry):
        first = pl.multiple_of(tile * LANES, LANES)
        for group in range(8):
            piece = sums[0][pl.ds(group * 1024 + first, LANES), :]
            for total in sums[1:]:
                piece = piece + total[pl.ds(group * 1024 + first, LANES), :]
            field_ref[:, group * 8 : (group + 1) * 8, pl.ds(first, LANES)] = piece.T.reshape(CH, 8, LANES)
        return carry

    lax.fori_loop(0, 8, turn, 0)

    for channel in range(CH):
        result = dot3(matrix_ref[channel].T[RLAT : RLAT + 16], field_ref[channel])
        to_north_ref[channel] = result[0:2, :CLON]
        to_south_ref[channel] = result[8:10, :CLON]


def observe(rows, cells, gram, backward):
    edge = jax.ShapeDtypeStruct((CH, 2, CLON), F32)
    return pl.pallas_call(
        observe_kernel,
        out_shape=(jax.ShapeDtypeStruct((CH, RLAT, 1024), F32), edge, edge),
        in_specs=[VM, pl.BlockSpec(memory_space=pltpu.HBM), VM, VM, VM],
        out_specs=(VM, VM, VM),
        scratch_shapes=[
            pltpu.VMEM((TILES, LANES), jnp.int32),
            pltpu.SMEM((TILES, LANES), jnp.int32),
            pltpu.VMEM((4, SLOTS, TILES, LANES), F32),
            pltpu.VMEM((4, SLOTS, 16, LANES), F32),
            pltpu.VMEM((4, SLOTS, 16, LANES), F32),
            pltpu.VMEM((SLOTS, TILES, LANES), F32),
            pltpu.SemaphoreType.DMA,
            pltpu.VMEM((CELL_ROWS, LANES), F32),
            pltpu.SemaphoreType.DMA,
        ]
        + [pltpu.VMEM((CELL_ROWS, LANES), F32)] * ACCS,
        compiler_params=params(46),
        name="observe",
    )(rows, cells, gram, jnp.asarray(pick_table(), BF16), backward)


def adjoint_kernel(field_ref, control_ref, matrix_ref, north_ref, south_ref, coupling_ref, local_ref):
    column = lax.broadcasted_iota(jnp.int32, (RLAT, LANES), 1)
    for inner in range(4):
        matrix = matrix_ref[inner]
        coupling = coupling_ref[pl.program_id(0) * 4 + inner]
        alpha_north = north_ref[inner, 2:3, 0:1] * coupling
        alpha_south = south_ref[inner, 2:3, 0:1] * coupling
        matrix = (
            matrix
            + jnp.where(column == 0, matrix[:, 64:65] * alpha_north, 0.0)
            + jnp.where(column == RLAT - 1, matrix[:, 72:73] * alpha_south, 0.0)
        )
        local_ref[inner] = control_ref[inner] + dot3(matrix.T[:RLAT], field_ref[inner])[:, :CLON]


def adjoint_diffusion(field, control, backward, from_north, from_south, coupling):
    def four(*shape):
        return pl.BlockSpec((4,) + shape, lambda i: (i, 0, 0))

    return pl.pallas_call(
        adjoint_kernel,
        grid=(4,),
        out_shape=jax.ShapeDtypeStruct((CH, RLAT, CLON), F32),
        in_specs=[four(RLAT, 1024), four(RLAT, CLON), four(RLAT, LANES), four(8, LANES), four(8, LANES), SM],
        out_specs=four(RLAT, CLON),
        cost_estimate=pl.CostEstimate(flops=6 * 64 * 64 * 16 * 1024, bytes_accessed=12 << 20, transcendentals=0),
        compiler_params=params(20),
        name="adjoint",
    )(field, control, backward, from_north, from_south, coupling)


ANY = pl.BlockSpec(memory_space=pl.ANY)
DFT_COST = pl.CostEstimate(flops=6 * 256 * 1024 * 1024, bytes_accessed=8 << 20, transcendentals=0)


def spectra_kernel(base, added, outputs, order_ref, local_any, north_ref, south_ref, mend_ref, head_ref, tail_ref, turn_ref, *refs):
    if added:
        add_ref, refs = refs[0], refs[1:]
    gradient_any, refs = refs[0], refs[1:]
    out_refs, (field_ref, fix_ref, in_semaphores, out_semaphores) = refs[:outputs], refs[outputs:]
    channels = [order_ref[base + i] for i in range(4)]
    loads = [
        pltpu.make_async_copy(local_any.at[channels[i]], field_ref.at[i], in_semaphores.at[i]) for i in range(4)
    ]
    for load in loads:
        load.start()
    for here, channel in enumerate(channels):
        mend = mend_ref[channel]
        north, south = north_ref[channel], south_ref[channel]
        fix_ref[here] = (
            mend[:, 0:1] * north[0:1]
            + mend[:, 1:2] * north[1:2]
            + mend[:, 2:3] * south[0:1]
            + mend[:, 3:4] * south[1:2]
        )
    for load in loads:
        load.wait()
    field_ref[...] = field_ref[...] + fix_ref[...]
    saves = [
        pltpu.make_async_copy(field_ref.at[i], gradient_any.at[channels[i]], out_semaphores.at[i]) for i in range(4)
    ]
    for save in saves:
        save.start()
    rows = 256
    head, tail = split(field_ref[...].reshape(rows, CLON))
    both = mm(jnp.concatenate([head, tail], axis=0), head_ref[...])
    result = both[:rows] + both[rows:] + mm(head, tail_ref[...])
    cos, sin = result[:, :KEEP], result[:, KEEP:]
    turn_cos, turn_sin = turn_ref[0:1, :], turn_ref[1:2, :]
    turned = (cos * turn_cos - sin * turn_sin, sin * turn_cos + cos * turn_sin)
    for part in range(2):
        lanes = slice(part * KEEP, (part + 1) * KEEP)
        for here in range(4):
            piece = turned[part][here * RLAT : (here + 1) * RLAT]
            if added:
                piece = piece + add_ref[here, :, lanes]
            out_refs[here * outputs // 4][here % (4 // outputs), :, lanes] = piece
    for save in saves:
        save.wait()


def spectra(base, order, local, north, south, mend, tables, turns, add=None):
    operands = [order, local, north, south, mend, *tables, turns]
    specs = [SM, ANY] + [VM] * 6
    outputs = 1
    if add is not None:
        operands.append(add)
        specs.append(VM)
        outputs = 2
    block = jax.ShapeDtypeStruct((4 // outputs, RLAT, 2 * KEEP), F32)
    return pl.pallas_call(
        functools.partial(spectra_kernel, base, add is not None, outputs),
        out_shape=(jax.ShapeDtypeStruct((CH, RLAT, CLON), F32),) + (block,) * outputs,
        in_specs=specs,
        out_specs=(ANY,) + (VM,) * outputs,
        scratch_shapes=[
            pltpu.VMEM((4, RLAT, CLON), F32),
            pltpu.VMEM((4, RLAT, CLON), F32),
            pltpu.SemaphoreType.DMA((4,)),
            pltpu.SemaphoreType.DMA((4,)),
        ],
        input_output_aliases={1: 0},
        cost_estimate=DFT_COST,
        compiler_params=params(24),
        name="spectra",
    )(*operands)


def synthesis_kernel(place, resumed, order_ref, head_ref, tail_ref, turn_ref, *refs):
    if resumed:
        refs = refs[1:]
    pieces, (out_any, field_ref, semaphores) = refs[:-3], refs[-3:]
    values = jnp.concatenate([piece[...] for piece in pieces], axis=0)
    cos, sin = values[:, :KEEP], values[:, KEEP:]
    turn_cos, turn_sin = turn_ref[0:1, :], turn_ref[1:2, :]
    values = jnp.concatenate([cos * turn_cos + sin * turn_sin, sin * turn_cos - cos * turn_sin], axis=1)
    head, tail = split(values)
    rows = 256
    both = mm(jnp.concatenate([head, tail], axis=0), head_ref[...])
    result = both[:rows] + both[rows:] + mm(head, tail_ref[...])
    field_ref[...] = result.reshape(4, RLAT, CLON)
    saves = [
        pltpu.make_async_copy(
            field_ref.at[pl.ds(2 * i, 2)], out_any.at[pl.ds(order_ref[place + 8 * (1 - i)], 2)], semaphores.at[i]
        )
        for i in range(2)
    ]
    for save in saves:
        save.start()
    for save in saves:
        save.wait()


def synthesis(place, order, tables, turns, pieces, before=None):
    operands = [order, *tables, turns]
    specs = [SM] + [VM] * 3
    if before is not None:
        operands.append(before)
        specs.append(ANY)
    return pl.pallas_call(
        functools.partial(synthesis_kernel, place, before is not None),
        out_shape=jax.ShapeDtypeStruct((CH, RLAT, CLON), F32),
        in_specs=specs + [VM] * len(pieces),
        out_specs=ANY,
        scratch_shapes=[pltpu.VMEM((4, RLAT, CLON), F32), pltpu.SemaphoreType.DMA((2,))],
        input_output_aliases={} if before is None else {4: 0},
        cost_estimate=DFT_COST,
        compiler_params=params(24),
        name="synthesis",
    )(*operands, *pieces)


def body(
    control,
    inverse,
    coupling,
    jacobian,
    error_weight,
    response,
    obs_values,
    obs_tile,
    obs_points,
    obs_weights,
    live_rows,
):
    lon = lax.axis_index("lon")
    ring, core = lon // 2, lon % 2
    partner = [(i, i ^ 1) for i in range(8)]
    onward = [(i, (i + 2) % 8) for i in range(8)]
    back = [(i, (i - 2) % 8) for i in range(8)]

    forward, backward, mend, north, south = bands(control, inverse, coupling)
    from_north, from_south = send_edges(north, south)

    routed = route(live_rows, obs_values, obs_tile, obs_points, obs_weights, jacobian, error_weight)
    rows = lax.all_to_all(routed, ("lat", "lon"), split_axis=0, concat_axis=0, tiled=True)

    state, cells = forward_diffusion(control, from_north, from_south, forward)
    gram = jnp.dot(jacobian * error_weight, jacobian.T, precision=EXACT)
    gram = jnp.repeat(jnp.repeat(gram, 8, axis=0), 8, axis=1)
    field, north, south = observe(
        rows.reshape(TILES, WORDS), cells.reshape(CELL_ROWS, LANES), gram, backward
    )
    edge_north, edge_south = send_edges(north, south)
    gradient = adjoint_diffusion(field, control, backward, from_north, from_south, coupling)

    head, tail = base_tables()
    tables = (jnp.asarray(head), jnp.asarray(tail))
    across_tables = (jnp.asarray(np.ascontiguousarray(head.T)), jnp.asarray(np.ascontiguousarray(tail.T)))
    turns = lax.dynamic_index_in_dim(jnp.asarray(turn_tables()), lon, 0, keepdims=False)
    chips = (ring + jnp.array([2, 1, 2, 3, 1, 3, 0, 0], jnp.int32)) % 4
    halves = jnp.array([0, 1, 1, 0, 0, 1, 0, 1], jnp.int32)
    order = jnp.concatenate([chips * 4 + 2 * (1 - core) + halves, chips * 4 + 2 * core + halves]).astype(jnp.int32)

    def analyse(base, gradient, add=None):
        return spectra(base, order, gradient, edge_north, edge_south, mend, tables, turns, add)

    def swap(piece):
        return lax.ppermute(piece, "lon", partner)

    gradient, ahead = analyse(0, gradient)
    ahead = swap(ahead)
    gradient, behind = analyse(4, gradient)
    behind = swap(behind)
    gradient, to_next, to_prior = analyse(8, gradient, ahead)
    from_prior = lax.ppermute(to_next, "lon", onward)
    from_next = lax.ppermute(to_prior, "lon", back)
    gradient, sides, own = analyse(12, gradient, behind)
    last_prior = lax.ppermute(sides[0] + from_prior[0], "lon", onward)
    last_next = lax.ppermute(sides[1] + from_next[0], "lon", back)
    wavenumber = jnp.arange(KEEP, dtype=jnp.int32)
    factor = jnp.where(wavenumber == 0, 1.0, 2.0).astype(F32) * response / NLON
    spectrum = jnp.concatenate(
        [own[0] + last_prior + from_next[1], own[1] + from_prior[1] + last_next]
    ) * jnp.concatenate([factor, factor])

    from_prior = lax.ppermute(spectrum, "lon", onward)
    from_next = lax.ppermute(spectrum, "lon", back)
    direction = synthesis(6, order, across_tables, turns, [spectrum, swap(spectrum)])
    from_prior, from_next, direction = lax.optimization_barrier((from_prior, from_next, direction))
    far_a = lax.ppermute(from_prior[:64], "lon", onward)
    far_b = lax.ppermute(from_next[64:], "lon", back)
    direction = synthesis(3, order, across_tables, turns, [from_prior, swap(from_prior)], direction)
    direction = synthesis(4, order, across_tables, turns, [from_next, swap(from_next)], direction)
    far_a, far_b, direction = lax.optimization_barrier((far_a, far_b, direction))
    direction = synthesis(0, order, across_tables, turns, [far_a, far_b, swap(far_a), swap(far_b)], direction)
    return (state, gradient, direction)


def solution(mesh):
    return jax.shard_map(
        body,
        mesh=mesh,
        in_specs=(
            P(None, "lat", "lon"),
            P("lat", None, None, None),
            P(),
            P(),
            P(),
            P(),
            P(("lat", "lon"), None),
            P(("lat", "lon"), None),
            P(("lat", "lon"), None),
            P(("lat", "lon"), None),
            P(("lat", "lon")),
        ),
        out_specs=(P(None, "lat", "lon"), P(None, "lat", "lon"), P(None, "lat", "lon")),
        check_vma=False,
    )
```
